32 devices in a mesh: freq: 4 (over y, x), shot: 8 (over z, core).
Axes of the slice: x: 2, y: 2, z: 4, core: 2. Of those that a mesh axis runs over, the one named last changes fastest.
Arguments:
- source_field: bfloat16 [8, 8, 2, 128, 4096], P('freq', 'shot'), may hold values from -6 to 6
- receiver_field: bfloat16 [8, 8, 2, 128, 4096], P('freq', 'shot'), may hold values from -6 to 6
- angular_freq: float32 [8], P('freq'), may hold values from 2 to 40
- x_correction: bfloat16 [8, 2, 128, 128], P('freq'), may hold values from -0.25 to 0.25
- y_correction: bfloat16 [8, 2, 128, 128], P('freq'), may hold values from -0.25 to 0.25
- velocity: float32 [8, 128, 4096], P('shot'), may hold values from -1.2 to 1.2
- slab_owner: int32 [2], replicated, may hold values from 0 to 7, as said below
- apertures: int32 [8, 2], P('shot'), may hold values from 0 to 31
- tile_order: int32 [32], replicated, may hold values from 0 to 31, each once
Outputs:
- source_out: bfloat16 [8, 8, 2, 128, 4096], P('freq', 'shot')
- receiver_out: bfloat16 [8, 8, 2, 128, 4096], P('freq', 'shot')
- image: float32 [32, 2, 16384], P('shot', None, 'freq')
The draws below stay inside these ranges and needn't reach their ends.
Inputs may be any that keep to these rules, and one draw needn't show every extreme that they name: `slab_owner`: the 2 entries are all different. `tile_order`: a permutation of all tiles.
All inputs are finite; a program needn't handle non-finite values.
Results may differ from the reference program's by a relative error of at most 0.0094.
Values sent between devices are 32-bit elements; how exact they have to be, the bound alone decides.
A program may use at most 128 MiB of HBM per device.

```python
import math
import jax
import jax.numpy as jnp
import numpy as np
from jax import lax

NX = 4096
YW = 128
BLOCK = 128
DEPTH = 2
APER = 2
FREQS = 8
SHOTS = 8
TILES = 32
TX = 128


def draw_slab_owner(key, part):
    key = jax.random.fold_in(key, 11)
    shuffle_key, place_key = jax.random.split(key)
    others = jax.random.permutation(shuffle_key, SHOTS - 1).astype(jnp.int32)
    others = jnp.concatenate([others, jnp.zeros((1,), jnp.int32)])
    place = jax.random.randint(place_key, (), 0, DEPTH).astype(jnp.int32)
    steps = jnp.arange(DEPTH, dtype=jnp.int32)
    before = others[steps]
    after = others[jnp.maximum(steps - 1, 0)]
    picked = jnp.where(steps < place, before, after)
    picked = jnp.where(steps == place, jnp.int32(SHOTS - 1), picked)
    return picked.astype(jnp.int32)


def place_ends(values, own_key, low, largest):
    longest = values.shape.index(max(values.shape))
    spots = []
    for shift in (0, 1):
        where = [jax.random.randint(jax.random.fold_in(own_key, axis), (), 0, length) for axis, length in enumerate(values.shape)]
        where[longest] = (where[longest] + shift) % values.shape[longest]
        spots.append(tuple(where))
    return values.at[spots[0]].set(low).at[spots[1]].set(largest)


def level_of(rng, dims, pieces, least, largest):
    loudness, own = 1.0, jax.random.fold_in(rng, 6)
    for axis_at, blocks in pieces:
        steps = jnp.exp(jax.random.uniform(jax.random.fold_in(own, axis_at), (blocks,), jnp.float32, least / len(pieces), largest / len(pieces)))
        loudness = loudness * jnp.repeat(steps, dims[axis_at] // blocks).reshape([-1 if axis == axis_at else 1 for axis in range(len(dims))])
    return loudness


def rank_bounds(count, slope):
    weights = [(1 << 20) // math.isqrt(standing ** slope) + 1 for standing in range(1, count + 1)]
    spread = 1 + sum(weights) // (1 << 30)
    return np.cumsum(np.array([max(1, weight // spread) for weight in weights]))


def ranked_ids(stream_key, dims, amount, skew):
    grid = rank_bounds(amount, skew)
    pick = jax.random.randint(jax.random.fold_in(stream_key, 1), dims, 0, int(grid[amount - 1]))
    rank = jnp.searchsorted(jnp.asarray(grid, jnp.int32), pick, side="right")
    return jax.random.permutation(jax.random.fold_in(stream_key, 2), amount)[rank].astype(jnp.int32)


def bell_draw(rng, extent, deviation, reach, cuts=(), held_as=jnp.bfloat16):
    loudness = level_of(rng, extent, cuts, -0.22, 0.18) if cuts else 1.0
    entries = jax.random.normal(rng, extent, jnp.float32) * deviation * loudness
    return jnp.minimum(jnp.maximum(entries, -reach), reach).astype(held_as)


def setup_inputs(seed: int = 0) -> dict:
    keys = jax.random.split(jax.random.key(seed), 10)
    return {
        "source_field": bell_draw(keys[0], (FREQS, SHOTS, 2, YW, NX), 1.0, 6.0, ((0, 4), (1, 8))),
        "receiver_field": bell_draw(keys[1], (FREQS, SHOTS, 2, YW, NX), 1.0, 6.0, ((0, 4), (1, 8))),
        "angular_freq": jnp.clip(jnp.exp(math.log(40.0) - 2.9957323 * jax.random.uniform(keys[2], (FREQS,), jnp.float32) ** level_of(keys[2], (FREQS,), ((0, 4),), -0.2, 0.2)), 2.0, 40.0),
        "x_correction": bell_draw(keys[3], (FREQS, 2, BLOCK, BLOCK), (4 * BLOCK) ** -0.5, 0.25, ((0, 4),)),
        "y_correction": bell_draw(keys[4], (FREQS, 2, BLOCK, BLOCK), (4 * BLOCK) ** -0.5, 0.25, ((0, 4),)),
        "velocity": bell_draw(keys[5], (SHOTS, YW, NX), 0.2, 1.2, ((0, 8),), jnp.float32),
        "slab_owner": draw_slab_owner(jax.random.fold_in(keys[9], 71), 0),
        "apertures": place_ends(ranked_ids(keys[7], (SHOTS, APER), TILES, 2), jax.random.fold_in(keys[7], 3), 0, TILES - 1).astype(jnp.int32),
        "tile_order": jax.random.permutation(keys[8], TILES).astype(jnp.int32),
    }


def lens(field, phase_angle, conj_sign):
    real_part = field[..., 0, :, :].astype(jnp.float32)
    imag_part = field[..., 1, :, :].astype(jnp.float32)
    cosine = jnp.cos(phase_angle)
    sine = conj_sign * jnp.sin(phase_angle)
    new_real = real_part * cosine - imag_part * sine
    new_imag = real_part * sine + imag_part * cosine
    return jnp.stack([new_real, new_imag], axis=-3).astype(jnp.bfloat16)


def sweep_x(field, correction, conj_sign):
    shape = field.shape
    width = correction.shape[-1]
    blocks = field.astype(jnp.float32).reshape(shape[:-1] + (shape[-1] // width, width))
    real_part = blocks[:, 0]
    imag_part = blocks[:, 1]
    c_real = correction[0].astype(jnp.float32)
    c_imag = correction[1].astype(jnp.float32)
    new_real = real_part + jnp.einsum('synk,kj->synj', real_part, c_real) - conj_sign * jnp.einsum('synk,kj->synj', imag_part, c_imag)
    new_imag = imag_part + jnp.einsum('synk,kj->synj', imag_part, c_real) + conj_sign * jnp.einsum('synk,kj->synj', real_part, c_imag)
    return jnp.stack([new_real, new_imag], axis=1).reshape(shape).astype(jnp.bfloat16)


def sweep_y(field, correction, conj_sign):
    shape = field.shape
    width = correction.shape[-1]
    blocks = field.astype(jnp.float32).reshape(shape[:2] + (shape[2] // width, width, shape[3]))
    real_part = blocks[:, 0]
    imag_part = blocks[:, 1]
    c_real = correction[0].astype(jnp.float32)
    c_imag = correction[1].astype(jnp.float32)
    new_real = real_part + jnp.einsum('snkx,kj->snjx', real_part, c_real) - conj_sign * jnp.einsum('snkx,kj->snjx', imag_part, c_imag)
    new_imag = imag_part + jnp.einsum('snkx,kj->snjx', imag_part, c_real) + conj_sign * jnp.einsum('snkx,kj->snjx', real_part, c_imag)
    return jnp.stack([new_real, new_imag], axis=1).reshape(shape).astype(jnp.bfloat16)


def reference(source_field, receiver_field, angular_freq, x_correction, y_correction, velocity, slab_owner, apertures, tile_order):
    slabs = [velocity[slab_owner[depth_step]] for depth_step in range(DEPTH)]

    def one_frequency(carry, inputs):
        source, receiver, angular, x_corr, y_corr = inputs
        totals = []
        for depth_step in range(DEPTH):
            phase_angle = angular * slabs[depth_step]
            source = sweep_y(sweep_x(lens(source, phase_angle, 1.0), x_corr, 1.0), y_corr, 1.0)
            receiver = sweep_y(sweep_x(lens(receiver, phase_angle, -1.0), x_corr, -1.0), y_corr, -1.0)
            image_term = source[:, 0].astype(jnp.float32) * receiver[:, 0].astype(jnp.float32) + source[:, 1].astype(jnp.float32) * receiver[:, 1].astype(jnp.float32)
            totals.append(carry[depth_step] + image_term)
        return tuple(totals), (source, receiver)

    start = tuple(jnp.zeros((SHOTS, YW, NX), jnp.float32) for depth_step in range(DEPTH))
    totals, outputs = lax.scan(one_frequency, start, (source_field, receiver_field, angular_freq, x_correction, y_correction))
    source_out, receiver_out = outputs
    match_table = (apertures[:, :, None] == tile_order[None, None, :]).astype(jnp.float32)
    shot_index = jnp.arange(SHOTS)[:, None]
    images = []
    for depth_step in range(DEPTH):
        image_term = totals[depth_step] / FREQS
        blocks = jnp.transpose(image_term.reshape(SHOTS, YW, TILES, TX), (0, 2, 1, 3))
        picked = blocks[shot_index, apertures]
        images.append(jnp.einsum('sap,sayx->pyx', match_table, picked, precision=lax.Precision.HIGHEST))
    image = jnp.stack(images, axis=1).reshape(TILES, DEPTH, YW * TX)
    return source_out, receiver_out, image
```

```python
import functools
import math

import jax
import jax.numpy as jnp
from jax import lax
from jax.experimental import pallas as pl
from jax.experimental.pallas import tpu as pltpu
from jax.sharding import PartitionSpec as P

DEPTH = 2
TILE_DEV = 4
CHUNK = 512
SIN = (4.44288292, -7.3082457, 3.60635441, -0.84611287, 0.10982695)
COS = (1.4142135, -6.97885099, 5.73946116, -1.88356292, 0.31069804)
F32 = jnp.float32
BF16 = jnp.bfloat16


def spread(shard, axis, root):
    mine = lax.axis_index(axis) == root
    return lax.psum(jnp.where(mine, shard, jnp.zeros_like(shard)), axis)


def horner(coefficients, z):
    total = jnp.full_like(z, coefficients[-1])
    for coefficient in coefficients[-2::-1]:
        total = total * z + coefficient
    return total


def cos_sin(turns):
    r = turns - jnp.round(turns)
    z = r * r
    half_sin = r * horner(SIN, z)
    half_cos = horner(COS, z)
    return 1.0 - half_sin * half_sin, half_sin * half_cos


def build_matrices(x_ref, y_ref, mx, my):
    for f in range(x_ref.shape[0]):
        xr, xi = x_ref[f, 0], x_ref[f, 1]
        yr = y_ref[f, 0].astype(F32).T.astype(BF16)
        yi = y_ref[f, 1].astype(F32).T.astype(BF16)
        for field in range(2):
            px, nx = (xi, -xi) if field == 0 else (-xi, xi)
            py, ny = (yi, -yi) if field == 0 else (-yi, yi)
            mx[f, field] = jnp.concatenate(
                [jnp.concatenate([xr, px], axis=1), jnp.concatenate([nx, xr], axis=1)], axis=0
            )
            my[f, field] = jnp.concatenate(
                [jnp.concatenate([yr, ny], axis=1), jnp.concatenate([py, yr], axis=1)], axis=0
            )


def step_field(re, im, cosine, sine, mx, my):
    height, width = re.shape
    re = re.astype(F32)
    im = im.astype(F32)
    lre = (re * cosine - im * sine).astype(BF16)
    lim = (re * sine + im * cosine).astype(BF16)
    tiles = width // 128
    rows = jnp.concatenate(
        [
            jnp.concatenate([lre[:, t * 128 : (t + 1) * 128], lim[:, t * 128 : (t + 1) * 128]], axis=1)
            for t in range(tiles)
        ],
        axis=0,
    )
    swept = (rows.astype(F32) + jnp.dot(rows, mx, preferred_element_type=F32)).astype(BF16)
    columns = jnp.concatenate(
        [
            jnp.concatenate([swept[t * height : (t + 1) * height, c : c + 128] for t in range(tiles)], axis=1)
            for c in (0, 128)
        ],
        axis=0,
    )
    out = (columns.astype(F32) + jnp.dot(my, columns, preferred_element_type=F32)).astype(BF16)
    return out[:height], out[height:]


def compute_kernel(
    freq_total, tiles_ref, freq_ref, source_ref, receiver_ref, x_ref, y_ref, slab_ref,
    source_out, receiver_out, term_ref, mx, my, kept,
):
    chunk = pl.program_id(0)

    @pl.when(chunk == 0)
    def _():
        build_matrices(x_ref, y_ref, mx, my)

    count = source_ref.shape[0]
    for f in range(count):
        scale = freq_ref[f] * (0.5 / math.pi)
        for d in range(DEPTH):
            cosine, sine = cos_sin(slab_ref[d] * scale)
            for field in range(2):
                first = (source_ref, receiver_ref)[field]
                if d == 0:
                    re, im = first[f, 0, 0], first[f, 0, 1]
                else:
                    re, im = kept[f, d - 1, field, 0], kept[f, d - 1, field, 1]
                re, im = step_field(
                    re, im, cosine, sine if field == 0 else -sine, mx[f, field], my[f, field]
                )
                kept[f, d, field, 0] = re
                kept[f, d, field, 1] = im
                if d == DEPTH - 1:
                    last = (source_out, receiver_out)[field]
                    last[f, 0, 0] = re
                    last[f, 0, 1] = im
    blocks = source_ref.shape[-1] // 128
    tile_width = term_ref.shape[-1]
    share = 128 // tile_width
    for a in range(term_ref.shape[0]):
        block = tiles_ref[a] // share - chunk * blocks
        place = tiles_ref[a] % share

        @pl.when(jnp.logical_and(block >= 0, block < blocks))
        def _():
            at = pl.ds(pl.multiple_of(block * 128, 128), 128)
            for d in range(DEPTH):
                total = jnp.zeros((term_ref.shape[2], 128), F32)
                for f in range(count):
                    for part in range(2):
                        total += kept[f, d, 0, part, :, at].astype(F32) * kept[f, d, 1, part, :, at].astype(F32)
                total = total * (1.0 / freq_total)
                picked = total[:, :tile_width]
                for p in range(1, share):
                    picked = jnp.where(place == p, total[:, p * tile_width : (p + 1) * tile_width], picked)
                term_ref[a, d] = picked


def compute(freq_total, tile_total, source, receiver, freq, xc, yc, slabs, tiles):
    count, _, _, height, width = source.shape
    tile_width = width // tile_total
    chunks = width // CHUNK
    field_spec = pl.BlockSpec((count, 1, 2, height, CHUNK), lambda i: (0, 0, 0, 0, i))
    smem = pl.BlockSpec(memory_space=pltpu.SMEM)
    whole = pl.BlockSpec(xc.shape, lambda i: (0, 0, 0, 0))
    aper = tiles.shape[0]
    return pl.pallas_call(
        functools.partial(compute_kernel, freq_total),
        grid=(chunks,),
        in_specs=[
            smem, smem, field_spec, field_spec, whole, whole,
            pl.BlockSpec((DEPTH, height, CHUNK), lambda i: (0, 0, i)),
        ],
        out_specs=[
            field_spec, field_spec,
            pl.BlockSpec((aper, DEPTH, height, tile_width), lambda i: (0, 0, 0, 0)),
        ],
        out_shape=[
            jax.ShapeDtypeStruct(source.shape, BF16),
            jax.ShapeDtypeStruct(receiver.shape, BF16),
            jax.ShapeDtypeStruct((aper, DEPTH, height, tile_width), F32),
        ],
        scratch_shapes=[
            pltpu.VMEM((count, 2, 256, 256), BF16),
            pltpu.VMEM((count, 2, 256, 256), BF16),
            pltpu.VMEM((count, DEPTH, 2, 2, height, CHUNK), BF16),
        ],
        compiler_params=pltpu.CompilerParams(vmem_limit_bytes=56 * 2**20),
        name="two_depth_steps",
    )(tiles, freq, source, receiver, xc, yc, slabs)


def local(
    source_field, receiver_field, angular_freq, x_correction, y_correction,
    velocity, slab_owner, apertures, tile_order,
):
    freq_total = angular_freq.shape[0] * lax.axis_size("freq")
    tile_ids = apertures[0]
    slabs = jnp.stack([spread(velocity[0], "shot", slab_owner[d]) for d in range(DEPTH)])
    source, receiver, terms = compute(
        freq_total, tile_order.shape[0], source_field, receiver_field, angular_freq, x_correction, y_correction, slabs, tile_ids
    )
    parts = lax.psum_scatter(terms, "freq", scatter_dimension=2, tiled=True)
    parts = parts.reshape(parts.shape[0], DEPTH, -1)
    every = lax.all_gather(parts, "shot", axis=0, tiled=True)
    ids = lax.all_gather(tile_ids, "shot", axis=0, tiled=True)
    mine = lax.dynamic_slice(tile_order, (lax.axis_index("shot") * TILE_DEV,), (TILE_DEV,))
    match = mine[:, None] == ids[None, :]
    image = jnp.sum(jnp.where(match[:, :, None, None], every[None], 0.0), axis=1)
    return source, receiver, image


def solution(mesh):
    in_specs = (
        P("freq", "shot", None, None, None),
        P("freq", "shot", None, None, None),
        P("freq"),
        P("freq", None, None, None),
        P("freq", None, None, None),
        P("shot", None, None),
        P(),
        P("shot", None),
        P(),
    )
    out_specs = (
        P("freq", "shot", None, None, None),
        P("freq", "shot", None, None, None),
        P("shot", None, "freq"),
    )
    return jax.shard_map(local, mesh=mesh, in_specs=in_specs, out_specs=out_specs, check_vma=False)
```

```python
import functools
import math

import jax
import jax.numpy as jnp
from jax import lax
from jax.experimental import pallas as pl
from jax.experimental.pallas import tpu as pltpu
from jax.sharding import PartitionSpec as P

DEPTH = 2
TILE_DEV = 4
CHUNK = 512
SIN = (4.44288292, -7.3082457, 3.60635441, -0.84611287, 0.10982695)
COS = (1.4142135, -6.97885099, 5.73946116, -1.88356292, 0.31069804)
F32 = jnp.float32
BF16 = jnp.bfloat16
MESH = pl.DeviceIdType.MESH
LAG = 2


def horner(coefficients, z):
    total = jnp.full_like(z, coefficients[-1])
    for coefficient in coefficients[-2::-1]:
        total = total * z + coefficient
    return total


def cos_sin(turns):
    r = turns - jnp.round(turns)
    z = r * r
    half_sin = r * horner(SIN, z)
    half_cos = horner(COS, z)
    return 1.0 - half_sin * half_sin, half_sin * half_cos


def build_matrices(x_ref, y_ref, mx, my):
    for f in range(x_ref.shape[0]):
        xr, xi = x_ref[f, 0], x_ref[f, 1]
        yr = y_ref[f, 0].astype(F32).T.astype(BF16)
        yi = y_ref[f, 1].astype(F32).T.astype(BF16)
        for field in range(2):
            px, nx = (xi, -xi) if field == 0 else (-xi, xi)
            py, ny = (yi, -yi) if field == 0 else (-yi, yi)
            mx[f, field] = jnp.concatenate(
                [jnp.concatenate([xr, px], axis=1), jnp.concatenate([nx, xr], axis=1)], axis=0
            )
            my[f, field] = jnp.concatenate(
                [jnp.concatenate([yr, ny], axis=1), jnp.concatenate([py, yr], axis=1)], axis=0
            )


def step_field(re, im, cosine, sine, mx, my):
    height, width = re.shape
    re = re.astype(F32)
    im = im.astype(F32)
    lre = (re * cosine - im * sine).astype(BF16)
    lim = (re * sine + im * cosine).astype(BF16)
    tiles = width // 128
    rows = jnp.concatenate(
        [
            jnp.concatenate([lre[:, t * 128 : (t + 1) * 128], lim[:, t * 128 : (t + 1) * 128]], axis=1)
            for t in range(tiles)
        ],
        axis=0,
    )
    swept = (rows.astype(F32) + jnp.dot(rows, mx, preferred_element_type=F32)).astype(BF16)
    columns = jnp.concatenate(
        [
            jnp.concatenate([swept[t * height : (t + 1) * height, c : c + 128] for t in range(tiles)], axis=1)
            for c in (0, 128)
        ],
        axis=0,
    )
    out = (columns.astype(F32) + jnp.dot(my, columns, preferred_element_type=F32)).astype(BF16)
    return out[:height], out[height:]


def compute_kernel(
    freq_total, tiles_ref, freq_ref, source_ref, receiver_ref, x_ref, y_ref, slab_ref,
    source_out, receiver_out, term_ref, mx, my, kept,
):
    chunk = pl.program_id(0)

    @pl.when(chunk == 0)
    def _():
        build_matrices(x_ref, y_ref, mx, my)

    count = source_ref.shape[0]
    for f in range(count):
        scale = freq_ref[f] * (0.5 / math.pi)
        for d in range(DEPTH):
            cosine, sine = cos_sin(slab_ref[d] * scale)
            for field in range(2):
                first = (source_ref, receiver_ref)[field]
                if d == 0:
                    re, im = first[f, 0, 0], first[f, 0, 1]
                else:
                    re, im = kept[f, d - 1, field, 0], kept[f, d - 1, field, 1]
                re, im = step_field(
                    re, im, cosine, sine if field == 0 else -sine, mx[f, field], my[f, field]
                )
                kept[f, d, field, 0] = re
                kept[f, d, field, 1] = im
                if d == DEPTH - 1:
                    last = (source_out, receiver_out)[field]
                    last[f, 0, 0] = re
                    last[f, 0, 1] = im
    blocks = source_ref.shape[-1] // 128
    tile_width = term_ref.shape[-1]
    share = 128 // tile_width
    for a in range(term_ref.shape[0]):
        block = tiles_ref[a] // share - chunk * blocks
        place = tiles_ref[a] % share

        @pl.when(jnp.logical_and(block >= 0, block < blocks))
        def _():
            at = pl.ds(pl.multiple_of(block * 128, 128), 128)
            for d in range(DEPTH):
                total = jnp.zeros((term_ref.shape[2], 128), F32)
                for f in range(count):
                    for part in range(2):
                        total += kept[f, d, 0, part, :, at].astype(F32) * kept[f, d, 1, part, :, at].astype(F32)
                total = total * (1.0 / freq_total)
                picked = total[:, :tile_width]
                for p in range(1, share):
                    picked = jnp.where(place == p, total[:, p * tile_width : (p + 1) * tile_width], picked)
                term_ref[a, d] = picked


def compute(freq_total, tile_total, source, receiver, freq, xc, yc, slabs, tiles):
    count, _, _, height, width = source.shape
    tile_width = width // tile_total
    chunks = width // CHUNK
    field_spec = pl.BlockSpec((count, 1, 2, height, CHUNK), lambda i: (0, 0, 0, 0, i))
    smem = pl.BlockSpec(memory_space=pltpu.SMEM)
    whole = pl.BlockSpec(xc.shape, lambda i: (0, 0, 0, 0))
    aper = tiles.shape[0]
    return pl.pallas_call(
        functools.partial(compute_kernel, freq_total),
        grid=(chunks,),
        in_specs=[
            smem, smem, field_spec, field_spec, whole, whole,
            pl.BlockSpec((DEPTH, height, CHUNK), lambda i: (0, 0, i)),
        ],
        out_specs=[
            field_spec, field_spec,
            pl.BlockSpec((aper, DEPTH, height, tile_width), lambda i: (0, 0, 0, 0)),
        ],
        out_shape=[
            jax.ShapeDtypeStruct(source.shape, BF16),
            jax.ShapeDtypeStruct(receiver.shape, BF16),
            jax.ShapeDtypeStruct((aper, DEPTH, height, tile_width), F32),
        ],
        scratch_shapes=[
            pltpu.VMEM((count, 2, 256, 256), BF16),
            pltpu.VMEM((count, 2, 256, 256), BF16),
            pltpu.VMEM((count, DEPTH, 2, 2, height, CHUNK), BF16),
        ],
        compiler_params=pltpu.CompilerParams(vmem_limit_bytes=56 * 2**20),
        name="two_depth_steps",
    )(tiles, freq, source, receiver, xc, yc, slabs)


def greet(devices, count):
    barrier = pltpu.get_barrier_semaphore()
    for there, device in devices:
        if there is None:
            pl.semaphore_signal(barrier, inc=1, device_id=device, device_id_type=MESH)
        else:

            @pl.when(there)
            def _(device=device):
                pl.semaphore_signal(barrier, inc=1, device_id=device, device_id_type=MESH)

    pl.semaphore_wait(barrier, count)


def remote(src, dst, send, recv, device):
    return pltpu.make_async_remote_copy(
        src_ref=src, dst_ref=dst, send_sem=send, recv_sem=recv, device_id=device, device_id_type=MESH
    )


def slab_kernel(
    freqs, shots, owner_ref, velocity_ref, out_ref,
    slabs, sibling_part, mine, up_out, up_in, down_out, down_in,
    pair_sem, up_sem, down_sem, plane_send, plane_recv, core_send, core_recv, out_sem,
):
    f = lax.axis_index("freq")
    s = lax.axis_index("shot")
    chain = shots // 2
    z = s // 2
    c = s % 2
    rows, width = slabs.shape[2], slabs.shape[3]
    chunks = width // CHUNK
    sibling = (f, z * 2 + 1 - c)
    above = (f, jnp.minimum(s + 2, shots - 2 + c))
    below = (f, jnp.maximum(s - 2, c))
    own = f * 2 + c
    others = [(lax.rem(f + j, freqs), s) for j in range(1, freqs)]
    has_below = z > 0
    has_above = z < chain - 1
    greet(
        [(None, sibling)] + [(None, o) for o in others] + [(has_above, above), (has_below, below)],
        freqs + has_above.astype(jnp.int32) + has_below.astype(jnp.int32),
    )

    def row_slice(index):
        return pl.ds(pl.multiple_of(index * rows, 8), rows)

    pair = remote(
        velocity_ref.at[0, row_slice(f * 2 + 1 - c)], sibling_part, pair_sem.at[0], pair_sem.at[1], sibling
    )
    pair.start()

    @pl.when(z == 0)
    def _():
        up_in[...] = jnp.zeros_like(up_in)

    @pl.when(z == chain - 1)
    def _():
        down_in[...] = jnp.zeros_like(down_in)

    pair.wait_recv()
    own_part = velocity_ref[0, row_slice(own)]
    other_part = sibling_part[...]
    for d in range(DEPTH):
        held = jnp.where(owner_ref[d] == s, own_part, jnp.zeros_like(own_part))
        mine[d] = jnp.where(owner_ref[d] == z * 2 + 1 - c, other_part, held)

    def at(k):
        return pl.ds(pl.multiple_of(k * CHUNK, CHUNK), CHUNK)

    def up_copy(k):
        return remote(
            up_out.at[:, :, at(k)], up_in.at[:, :, at(k)], up_sem.at[0, k], up_sem.at[1, k], above
        )

    def down_copy(k):
        return remote(
            down_out.at[:, :, at(k)], down_in.at[:, :, at(k)], down_sem.at[0, k], down_sem.at[1, k], below
        )

    def plane_copy(j, k):
        place = slabs.at[:, own, :, at(k)]
        return remote(place, place, plane_send.at[j - 1, k], plane_recv.at[j - 1, k], others[j - 1])

    def core_copy(j, k):
        place = slabs.at[:, lax.rem(f + freqs - j, freqs) * 2 + c, :, at(k)]
        return remote(place, place, core_send.at[j, k], core_recv.at[j, k], sibling)

    def arrived(j, k):
        place = slabs.at[:, lax.rem(f + freqs - j, freqs) * 2 + c, :, at(k)]
        return remote(place, place, plane_send.at[j - 1, k], plane_recv.at[j - 1, k], others[j - 1])

    def core_arrived(j, k):
        place = slabs.at[:, lax.rem(f + freqs - j, freqs) * 2 + 1 - c, :, at(k)]
        return remote(place, place, core_send.at[j, k], core_recv.at[j, k], sibling)

    def go_up(k):
        @pl.when(has_below)
        def _():
            up_copy(k).wait_recv()

        @pl.when(has_above)
        def _():
            up_out[:, :, at(k)] = up_in[:, :, at(k)] + mine[:, :, at(k)]
            up_copy(k).start()

    def go_down(k):
        @pl.when(has_above)
        def _():
            down_copy(k).wait_recv()

        @pl.when(has_below)
        def _():
            down_out[:, :, at(k)] = down_in[:, :, at(k)] + mine[:, :, at(k)]
            down_copy(k).start()

    lower = z < chain // 2
    upper = z >= chain // 2

    def out_copy(k):
        return pltpu.make_async_copy(slabs.at[:, :, :, at(k)], out_ref.at[:, :, :, at(k)], out_sem.at[k])

    def step(i, carry):
        @pl.when(i < chunks)
        def _():
            @pl.when(lower)
            def _():
                go_up(i)

            @pl.when(upper)
            def _():
                go_down(i)

        @pl.when(jnp.logical_and(i >= LAG, i < chunks + LAG))
        def _():
            k = i - LAG

            @pl.when(lower)
            def _():
                go_down(k)

            @pl.when(upper)
            def _():
                go_up(k)

            slabs[:, own, :, at(k)] = up_in[:, :, at(k)] + mine[:, :, at(k)] + down_in[:, :, at(k)]
            for j in range(1, freqs):
                plane_copy(j, k).start()
            core_copy(0, k).start()

        @pl.when(jnp.logical_and(i >= LAG + 1, i < chunks + LAG + 1))
        def _():
            k = i - LAG - 1
            for j in range(1, freqs):
                arrived(j, k).wait_recv()
                core_copy(j, k).start()

        @pl.when(i >= LAG + 2)
        def _():
            k = i - LAG - 2
            for j in range(freqs):
                core_arrived(j, k).wait_recv()
            out_copy(k).start()

        return carry

    lax.fori_loop(0, chunks + LAG + 2, step, 0)
    pair.wait_send()

    def drain(k, carry):
        @pl.when(has_above)
        def _():
            up_copy(k).wait_send()

        @pl.when(has_below)
        def _():
            down_copy(k).wait_send()

        for j in range(1, freqs):
            plane_copy(j, k).wait_send()
        for j in range(freqs):
            core_copy(j, k).wait_send()
        out_copy(k).wait()
        return carry

    lax.fori_loop(0, chunks, drain, 0)


def exchange_slabs(freqs, shots, owners, velocity):
    _, height, width = velocity.shape
    rows = height // (2 * freqs)
    chunks = width // CHUNK
    strip = pltpu.VMEM((DEPTH, rows, width), F32)
    dma = pltpu.SemaphoreType.DMA
    slabs = pl.pallas_call(
        functools.partial(slab_kernel, freqs, shots),
        in_specs=[pl.BlockSpec(memory_space=pltpu.SMEM), pl.BlockSpec(memory_space=pltpu.VMEM)],
        out_specs=pl.BlockSpec(memory_space=pl.ANY),
        out_shape=jax.ShapeDtypeStruct((DEPTH, 2 * freqs, rows, width), F32),
        scratch_shapes=[
            pltpu.VMEM((DEPTH, 2 * freqs, rows, width), F32),
            pltpu.VMEM((rows, width), F32),
            strip, strip, strip, strip, strip,
            dma((2,)), dma((2, chunks)), dma((2, chunks)),
            dma((freqs - 1, chunks)), dma((freqs - 1, chunks)),
            dma((freqs, chunks)), dma((freqs, chunks)), dma((chunks,)),
        ],
        compiler_params=pltpu.CompilerParams(
            collective_id=0, has_side_effects=True, vmem_limit_bytes=48 * 2**20
        ),
        name="exchange_slabs",
    )(owners, velocity)
    return slabs.reshape(DEPTH, height, width)


def image_kernel(
    freqs, shots, ids_ref, order_ref, term_ref, out_ref,
    landed, gathered, sum_send, sum_recv, shot_send, shot_recv, core_send, core_recv,
):
    f = lax.axis_index("freq")
    s = lax.axis_index("shot")
    chain = shots // 2
    z = s // 2
    c = s % 2
    aper = term_ref.shape[0]
    rows = out_ref.shape[2]
    sibling = (f, z * 2 + 1 - c)
    others = [(lax.rem(f + j, freqs), s) for j in range(1, freqs)]
    chips = [lax.rem(z + j, chain) * 2 + c for j in range(chain)]
    greet(
        [(None, sibling)] + [(None, o) for o in others] + [(None, (f, chip)) for chip in chips[1:]],
        freqs + chain - 1,
    )

    def row_slice(index):
        return pl.ds(pl.multiple_of(index * rows, 8), rows)

    sums = [
        remote(
            term_ref.at[:, :, row_slice(others[j - 1][0])], landed.at[j - 1],
            sum_send.at[j - 1], sum_recv.at[j - 1], others[j - 1],
        )
        for j in range(1, freqs)
    ]
    for copy in sums:
        copy.start()
    for a in range(aper):
        gathered[s, a, DEPTH * rows :] = jnp.full((8, term_ref.shape[3]), ids_ref[a].astype(F32))
    total = term_ref[:, :, row_slice(f)]
    for j in range(1, freqs):
        sums[j - 1].wait_recv()
        total = total + landed[j - 1]
    gathered[s, :, : DEPTH * rows] = total.reshape(aper, DEPTH * rows, -1)

    place = gathered.at[s]
    sends = [
        remote(place, place, shot_send.at[j - 1], shot_recv.at[j - 1], (f, chips[j])) for j in range(1, chain)
    ]
    for copy in sends:
        copy.start()
    forwards = []
    for j in range(chain):
        source = gathered.at[lax.rem(z + chain - j, chain) * 2 + c]
        if j:
            remote(source, source, shot_send.at[j - 1], shot_recv.at[j - 1], (f, chips[j])).wait_recv()
        forwards.append(remote(source, source, core_send.at[j], core_recv.at[j], sibling))
        forwards[-1].start()
    for j in range(chain):
        landing = gathered.at[lax.rem(z + chain - j, chain) * 2 + 1 - c]
        remote(landing, landing, core_send.at[j], core_recv.at[j], sibling).wait_recv()

    for p in range(TILE_DEV):
        wanted = order_ref[s * TILE_DEV + p].astype(F32)
        picked = jnp.zeros((DEPTH * rows // 8, 8, term_ref.shape[3]), F32)
        for other in range(shots):
            for a in range(aper):
                hit = gathered[other, a, DEPTH * rows :] == wanted
                value = gathered[other, a, : DEPTH * rows].reshape(picked.shape)
                picked += jnp.where(hit[None], value, 0.0)
        out_ref[p] = picked.reshape(DEPTH, rows, -1)
    for copy in sums + sends + forwards:
        copy.wait_send()


def exchange_image(freqs, shots, ids, order, terms):
    aper, _, height, tile_width = terms.shape
    rows = height // freqs
    chain = shots // 2
    smem = pl.BlockSpec(memory_space=pltpu.SMEM)
    vmem = pl.BlockSpec(memory_space=pltpu.VMEM)
    dma = pltpu.SemaphoreType.DMA
    image = pl.pallas_call(
        functools.partial(image_kernel, freqs, shots),
        in_specs=[smem, smem, vmem],
        out_specs=vmem,
        out_shape=jax.ShapeDtypeStruct((TILE_DEV, DEPTH, rows, tile_width), F32),
        scratch_shapes=[
            pltpu.VMEM((freqs - 1, aper, DEPTH, rows, tile_width), F32),
            pltpu.VMEM((shots, aper, DEPTH * rows + 8, tile_width), F32),
            dma((freqs - 1,)), dma((freqs - 1,)), dma((chain - 1,)), dma((chain - 1,)),
            dma((chain,)), dma((chain,)),
        ],
        compiler_params=pltpu.CompilerParams(
            collective_id=1, has_side_effects=True, vmem_limit_bytes=48 * 2**20
        ),
        name="exchange_image",
    )(ids, order, terms)
    return image.reshape(TILE_DEV, DEPTH, rows * tile_width)


def local(
    freqs, shots, source_field, receiver_field, angular_freq, x_correction, y_correction,
    velocity, slab_owner, apertures, tile_order,
):
    tile_ids = apertures[0]
    slabs = exchange_slabs(freqs, shots, slab_owner, velocity)
    source, receiver, terms = compute(
        angular_freq.shape[0] * freqs, tile_order.shape[0],
        source_field, receiver_field, angular_freq, x_correction, y_correction, slabs, tile_ids,
    )
    return source, receiver, exchange_image(freqs, shots, tile_ids, tile_order, terms)


def solution(mesh):
    in_specs = (
        P("freq", "shot", None, None, None),
        P("freq", "shot", None, None, None),
        P("freq"),
        P("freq", None, None, None),
        P("freq", None, None, None),
        P("shot", None, None),
        P(),
        P("shot", None),
        P(),
    )
    out_specs = (
        P("freq", "shot", None, None, None),
        P("freq", "shot", None, None, None),
        P("shot", None, "freq"),
    )
    body = functools.partial(local, mesh.shape["freq"], mesh.shape["shot"])
    return jax.shard_map(body, mesh=mesh, in_specs=in_specs, out_specs=out_specs, check_vma=False)
```

```python
import functools
import math

import jax
import jax.numpy as jnp
from jax import lax
from jax.experimental import pallas as pl
from jax.experimental.pallas import tpu as pltpu
from jax.sharding import PartitionSpec as P

DEPTH = 2
TILE_DEV = 4
CHUNK = 256
LAST_CHUNK = 512
SIN = (4.44288292, -7.3082457, 3.60635441, -0.84611287, 0.10982695)
COS = (1.4142135, -6.97885099, 5.73946116, -1.88356292, 0.31069804)
F32 = jnp.float32
BF16 = jnp.bfloat16
MESH = pl.DeviceIdType.MESH
LAG = 2
PLANE_LAG = LAG + 3
CORE_LAG = PLANE_LAG + 1


def horner(coefficients, z):
    total = jnp.full_like(z, coefficients[-1])
    for coefficient in coefficients[-2::-1]:
        total = total * z + coefficient
    return total


def cos_sin(turns):
    r = turns - jnp.round(turns)
    z = r * r
    half_sin = r * horner(SIN, z)
    half_cos = horner(COS, z)
    return 1.0 - half_sin * half_sin, half_sin * half_cos


def pair_matrix(real, below_left, above_right):
    return jnp.concatenate(
        [jnp.concatenate([real, above_right], axis=1), jnp.concatenate([below_left, real], axis=1)], axis=0
    )


def x_matrix(x_ref, f):
    return pair_matrix(x_ref[f, 0], -x_ref[f, 1], x_ref[f, 1])


def y_matrix(y_ref, f):
    real = y_ref[f, 0].astype(F32).T.astype(BF16)
    imag = y_ref[f, 1].astype(F32).T.astype(BF16)
    return pair_matrix(real, imag, -imag)


def sweep_x(re, im, mx):
    rows = jnp.concatenate(
        [
            jnp.concatenate([re[:, t : t + 128], im[:, t : t + 128]], axis=1)
            for t in range(0, re.shape[1], 128)
        ],
        axis=0,
    )
    swept = (rows.astype(F32) + jnp.dot(rows, mx, preferred_element_type=F32)).astype(BF16)
    height = re.shape[0]
    return [
        jnp.concatenate([swept[t : t + height, c : c + 128] for t in range(0, swept.shape[0], height)], axis=1)
        for c in (0, 128)
    ]


def sweep_y(re, im, my):
    columns = jnp.concatenate([re, im], axis=0)
    out = columns.astype(F32) + jnp.dot(my, columns, preferred_element_type=F32)
    return out[: re.shape[0]], out[re.shape[0] :]


def last_kernel(
    freq_total, ids_ref, y_ref, source_ref, receiver_ref, first_source, first_receiver, half_source, half_receiver,
    source_out, receiver_out, term_ref, my, tiles, tile_sem,
):
    step = pl.program_id(0)
    aper = term_ref.shape[0]
    tile_width = term_ref.shape[-1]
    share = 128 // tile_width
    whole = ((first_source, first_receiver), (half_source, half_receiver))

    def loads(a):
        at = pl.ds(pl.multiple_of(ids_ref[a] // share * 128, 128), 128)
        return [
            pltpu.make_async_copy(
                whole[d][field].at[:, 0, :, :, at], tiles.at[a, d, field], tile_sem.at[a, d, field]
            )
            for d in range(DEPTH)
            for field in range(2)
        ]

    @pl.when(step == 0)
    def _():
        for a in range(aper):
            for load in loads(a):
                load.start()
        for f in range(y_ref.shape[0]):
            my[f] = y_matrix(y_ref, f)

    for f in range(source_ref.shape[0]):
        re, im = sweep_y(source_ref[f, 0, 0], source_ref[f, 0, 1], my[f])
        source_out[f, 0, 0] = re.astype(BF16)
        source_out[f, 0, 1] = im.astype(BF16)
        re, im = sweep_y(receiver_ref[f, 0, 0], receiver_ref[f, 0, 1], my[f])
        receiver_out[f, 0, 0] = re.astype(BF16)
        receiver_out[f, 0, 1] = (-im).astype(BF16)

    @pl.when(step == 1)
    def _():
        for a in range(aper):
            for load in loads(a):
                load.wait()
            place = ids_ref[a] % share
            for d in range(DEPTH):
                total = jnp.zeros((term_ref.shape[2], 128), F32)
                for f in range(source_ref.shape[0]):
                    re, im = [
                        jnp.concatenate([tiles[a, d, field, f, part] for field in range(2)], axis=1)
                        for part in range(2)
                    ]
                    if d == DEPTH - 1:
                        re, im = [value.astype(BF16) for value in sweep_y(re, im, my[f])]
                    re, im = re.astype(F32), im.astype(F32)
                    total += re[:, :128] * re[:, 128:] - im[:, :128] * im[:, 128:]
                total = total * (1.0 / freq_total)
                picked = total[:, :tile_width]
                for p in range(1, share):
                    picked = jnp.where(place == p, total[:, p * tile_width : (p + 1) * tile_width], picked)
                term_ref[a, d] = picked


def last_sweep(freq_total, tile_total, ids, yc, first_source, first_receiver, source, receiver):
    count, _, _, height, width = source.shape
    aper = ids.shape[0]
    spec = pl.BlockSpec((count, 1, 2, height, LAST_CHUNK), lambda i: (0, 0, 0, 0, i))
    shape = jax.ShapeDtypeStruct(source.shape, BF16)
    term = (aper, DEPTH, height, width // tile_total)
    anywhere = pl.BlockSpec(memory_space=pl.ANY)
    return pl.pallas_call(
        functools.partial(last_kernel, freq_total),
        grid=(width // LAST_CHUNK,),
        in_specs=[
            pl.BlockSpec(memory_space=pltpu.SMEM), pl.BlockSpec(yc.shape, lambda i: (0, 0, 0, 0)),
            spec, spec, anywhere, anywhere, anywhere, anywhere,
        ],
        out_specs=[spec, spec, pl.BlockSpec(term, lambda i: (0, 0, 0, 0))],
        out_shape=[shape, shape, jax.ShapeDtypeStruct(term, F32)],
        scratch_shapes=[
            pltpu.VMEM((count, 256, 256), BF16),
            pltpu.VMEM((aper, DEPTH, 2, count, 2, height, 128), BF16),
            pltpu.SemaphoreType.DMA((aper, DEPTH, 2)),
        ],
        compiler_params=pltpu.CompilerParams(vmem_limit_bytes=48 * 2**20),
        name="last_sweep",
    )(ids, yc, source, receiver, first_source, first_receiver, source, receiver)


def greet(devices, count):
    barrier = pltpu.get_barrier_semaphore()
    for there, device in devices:
        if there is None:
            pl.semaphore_signal(barrier, inc=1, device_id=device, device_id_type=MESH)
        else:

            @pl.when(there)
            def _(device=device):
                pl.semaphore_signal(barrier, inc=1, device_id=device, device_id_type=MESH)

    pl.semaphore_wait(barrier, count)


def remote(src, dst, send, recv, device):
    return pltpu.make_async_remote_copy(
        src_ref=src, dst_ref=dst, send_sem=send, recv_sem=recv, device_id=device, device_id_type=MESH
    )


def slab_kernel(
    freqs, shots, owner_ref, freq_ref, velocity_ref, source_ref, receiver_ref, x_ref, y_ref,
    source_first, receiver_first, source_out, receiver_out,
    slabs, own_part, sibling_part, mine, up_out, up_in, down_out, down_in, fields, stage, mx, my,
    pair_sem, up_sem, down_sem, plane_send, plane_recv, core_send, core_recv, in_sem, out_sem,
):
    f = lax.axis_index("freq")
    s = lax.axis_index("shot")
    chain = shots // 2
    z = s // 2
    c = s % 2
    rows, width = slabs.shape[2], slabs.shape[3]
    chunks = width // CHUNK
    sibling = (f, z * 2 + 1 - c)
    above = (f, jnp.minimum(s + 2, shots - 2 + c))
    below = (f, jnp.maximum(s - 2, c))
    own = f * 2 + c
    field_refs = (source_ref, receiver_ref)
    out_refs = (source_first, receiver_first, source_out, receiver_out)
    count, height = source_ref.shape[0], source_ref.shape[3]
    loads = [
        pltpu.make_async_copy(field_refs[i].at[:, 0], fields.at[i], in_sem.at[i]) for i in range(2)
    ]
    others = [(lax.rem(f + j, freqs), s) for j in range(1, freqs)]
    has_below = z > 0
    has_above = z < chain - 1
    greet(
        [(None, sibling)] + [(None, o) for o in others] + [(has_above, above), (has_below, below)],
        freqs + has_above.astype(jnp.int32) + has_below.astype(jnp.int32),
    )

    def row_slice(index):
        return pl.ds(pl.multiple_of(index * rows, 8), rows)

    pair = remote(
        velocity_ref.at[0, row_slice(f * 2 + 1 - c)], sibling_part, pair_sem.at[0], pair_sem.at[1], sibling
    )
    pair.start()
    own_load = pltpu.make_async_copy(velocity_ref.at[0, row_slice(own)], own_part, in_sem.at[2])
    own_load.start()
    for load in loads:
        load.start()
    for i in range(count):
        mx[i] = x_matrix(x_ref, i)
        my[i] = y_matrix(y_ref, i)

    @pl.when(z == 0)
    def _():
        up_in[...] = jnp.zeros_like(up_in)

    @pl.when(z == chain - 1)
    def _():
        down_in[...] = jnp.zeros_like(down_in)

    own_load.wait()
    pair.wait_recv()
    here = own_part[...]
    there = sibling_part[...]
    for d in range(DEPTH):
        held = jnp.where(owner_ref[d] == s, here, jnp.zeros_like(here))
        mine[d] = jnp.where(owner_ref[d] == z * 2 + 1 - c, there, held)

    def at(k):
        return pl.ds(pl.multiple_of(k * CHUNK, CHUNK), CHUNK)

    def up_copy(k):
        return remote(
            up_out.at[:, :, at(k)], up_in.at[:, :, at(k)], up_sem.at[0, k], up_sem.at[1, k], above
        )

    def down_copy(k):
        return remote(
            down_out.at[:, :, at(k)], down_in.at[:, :, at(k)], down_sem.at[0, k], down_sem.at[1, k], below
        )

    def plane_copy(j, k):
        place = slabs.at[:, own, :, at(k)]
        return remote(place, place, plane_send.at[j - 1, k], plane_recv.at[j - 1, k], others[j - 1])

    def core_copy(j, k):
        place = slabs.at[:, lax.rem(f + freqs - j, freqs) * 2 + c, :, at(k)]
        return remote(place, place, core_send.at[j, k], core_recv.at[j, k], sibling)

    def arrived(j, k):
        place = slabs.at[:, lax.rem(f + freqs - j, freqs) * 2 + c, :, at(k)]
        return remote(place, place, plane_send.at[j - 1, k], plane_recv.at[j - 1, k], others[j - 1])

    def core_arrived(j, k):
        place = slabs.at[:, lax.rem(f + freqs - j, freqs) * 2 + 1 - c, :, at(k)]
        return remote(place, place, core_send.at[j, k], core_recv.at[j, k], sibling)

    def go_up(k):
        @pl.when(has_below)
        def _():
            up_copy(k).wait_recv()

        @pl.when(has_above)
        def _():
            up_out[:, :, at(k)] = up_in[:, :, at(k)] + mine[:, :, at(k)]
            up_copy(k).start()

    def go_down(k):
        @pl.when(has_above)
        def _():
            down_copy(k).wait_recv()

        @pl.when(has_below)
        def _():
            down_out[:, :, at(k)] = down_in[:, :, at(k)] + mine[:, :, at(k)]
            down_copy(k).start()

    lower = z < chain // 2
    upper = z >= chain // 2

    def out_copy(i, k):
        held = fields if i < 2 else stage
        return pltpu.make_async_copy(
            held.at[i % 2, :, :, :, at(k)], out_refs[i].at[:, 0, :, :, at(k)], out_sem.at[i, k]
        )

    def compute(k):
        for i in range(count):
            scale = freq_ref[i] * (0.5 / math.pi)
            cosine, sine = cos_sin(slabs[0, :, :, at(k)].reshape(height, CHUNK) * scale)
            sre, sim, rre, rim = [
                fields[field, i, part, :, at(k)].astype(F32) for field in range(2) for part in range(2)
            ]
            re = jnp.concatenate([sre * cosine - sim * sine, rre * cosine + rim * sine], axis=1)
            im = jnp.concatenate([sre * sine + sim * cosine, rre * sine - rim * cosine], axis=1)
            re, im = sweep_y(*sweep_x(re.astype(BF16), im.astype(BF16), mx[i]), my[i])
            re, im = re.astype(BF16), im.astype(BF16)
            for field in range(2):
                fields[field, i, 0, :, at(k)] = re[:, field * CHUNK : (field + 1) * CHUNK]
                fields[field, i, 1, :, at(k)] = im[:, field * CHUNK : (field + 1) * CHUNK]
            cosine, sine = cos_sin(slabs[1, :, :, at(k)].reshape(height, CHUNK) * scale)
            cosine = jnp.concatenate([cosine, cosine], axis=1)
            sine = jnp.concatenate([sine, sine], axis=1)
            re, im = re.astype(F32), im.astype(F32)
            re, im = sweep_x(
                (re * cosine - im * sine).astype(BF16), (re * sine + im * cosine).astype(BF16), mx[i]
            )
            for field in range(2):
                stage[field, i, 0, :, at(k)] = re[:, field * CHUNK : (field + 1) * CHUNK]
                stage[field, i, 1, :, at(k)] = im[:, field * CHUNK : (field + 1) * CHUNK]

    def step(i, carry):
        @pl.when(i < chunks)
        def _():
            @pl.when(lower)
            def _():
                go_up(i)

            @pl.when(upper)
            def _():
                go_down(i)

        @pl.when(jnp.logical_and(i >= LAG, i < chunks + LAG))
        def _():
            k = i - LAG

            @pl.when(lower)
            def _():
                go_down(k)

            @pl.when(upper)
            def _():
                go_up(k)

            slabs[:, own, :, at(k)] = up_in[:, :, at(k)] + mine[:, :, at(k)] + down_in[:, :, at(k)]
            for j in range(1, freqs):
                plane_copy(j, k).start()
            core_copy(0, k).start()

        @pl.when(jnp.logical_and(i >= PLANE_LAG, i < chunks + PLANE_LAG))
        def _():
            k = i - PLANE_LAG
            for j in range(1, freqs):
                arrived(j, k).wait_recv()
                core_copy(j, k).start()

        @pl.when(i == CORE_LAG)
        def _():
            for load in loads:
                load.wait()

        @pl.when(i >= CORE_LAG)
        def _():
            k = i - CORE_LAG
            for j in range(freqs):
                core_arrived(j, k).wait_recv()
            compute(k)
            for out in range(4):
                out_copy(out, k).start()

        return carry

    lax.fori_loop(0, chunks + CORE_LAG, step, 0)
    pair.wait_send()

    def drain(k, carry):
        @pl.when(has_above)
        def _():
            up_copy(k).wait_send()

        @pl.when(has_below)
        def _():
            down_copy(k).wait_send()

        for j in range(1, freqs):
            plane_copy(j, k).wait_send()
        for j in range(freqs):
            core_copy(j, k).wait_send()
        for out in range(4):
            out_copy(out, k).wait()
        return carry

    lax.fori_loop(0, chunks, drain, 0)


def exchange_slabs(freqs, shots, owners, freq, velocity, source, receiver, xc, yc):
    _, height, width = velocity.shape
    count = source.shape[0]
    rows = height // (2 * freqs)
    chunks = width // CHUNK
    vmem = pl.BlockSpec(memory_space=pltpu.VMEM)
    smem = pl.BlockSpec(memory_space=pltpu.SMEM)
    anywhere = pl.BlockSpec(memory_space=pl.ANY)
    strip = pltpu.VMEM((DEPTH, rows, width), F32)
    field = pltpu.VMEM((2, count, 2, height, width), BF16)
    matrix = pltpu.VMEM((count, 256, 256), BF16)
    dma = pltpu.SemaphoreType.DMA
    shape = jax.ShapeDtypeStruct(source.shape, BF16)
    return pl.pallas_call(
        functools.partial(slab_kernel, freqs, shots),
        in_specs=[smem, smem, anywhere, anywhere, anywhere, vmem, vmem],
        out_specs=[anywhere] * 4,
        out_shape=[shape] * 4,
        scratch_shapes=[
            pltpu.VMEM((DEPTH, 2 * freqs, rows, width), F32),
            pltpu.VMEM((rows, width), F32),
            pltpu.VMEM((rows, width), F32),
            strip, strip, strip, strip, strip, field, field, matrix, matrix,
            dma((2,)), dma((2, chunks)), dma((2, chunks)),
            dma((freqs - 1, chunks)), dma((freqs - 1, chunks)),
            dma((freqs, chunks)), dma((freqs, chunks)), dma((3,)), dma((4, chunks)),
        ],
        compiler_params=pltpu.CompilerParams(
            collective_id=0, has_side_effects=True, vmem_limit_bytes=56 * 2**20
        ),
        name="slabs_and_sweeps",
    )(owners, freq, velocity, source, receiver, xc, yc)


def image_kernel(
    freqs, shots, ids_ref, order_ref, term_ref, out_ref,
    landed, gathered, sum_send, sum_recv, shot_send, shot_recv, core_send, core_recv,
):
    f = lax.axis_index("freq")
    s = lax.axis_index("shot")
    chain = shots // 2
    z = s // 2
    c = s % 2
    aper = term_ref.shape[0]
    rows = out_ref.shape[2]
    sibling = (f, z * 2 + 1 - c)
    others = [(lax.rem(f + j, freqs), s) for j in range(1, freqs)]
    chips = [lax.rem(z + j, chain) * 2 + c for j in range(chain)]
    greet(
        [(None, sibling)] + [(None, o) for o in others] + [(None, (f, chip)) for chip in chips[1:]],
        freqs + chain - 1,
    )

    def row_slice(index):
        return pl.ds(pl.multiple_of(index * rows, 8), rows)

    sums = [
        remote(
            term_ref.at[:, :, row_slice(others[j - 1][0])], landed.at[j - 1],
            sum_send.at[j - 1], sum_recv.at[j - 1], others[j - 1],
        )
        for j in range(1, freqs)
    ]
    for copy in sums:
        copy.start()
    for a in range(aper):
        gathered[s, a, DEPTH * rows :] = jnp.full((8, term_ref.shape[3]), ids_ref[a].astype(F32))
    total = term_ref[:, :, row_slice(f)]
    for j in range(1, freqs):
        sums[j - 1].wait_recv()
        total = total + landed[j - 1]
    gathered[s, :, : DEPTH * rows] = total.reshape(aper, DEPTH * rows, -1)

    place = gathered.at[s]
    sends = [
        remote(place, place, shot_send.at[j - 1], shot_recv.at[j - 1], (f, chips[j])) for j in range(1, chain)
    ]
    for copy in sends:
        copy.start()
    forwards = []
    for j in range(chain):
        source = gathered.at[lax.rem(z + chain - j, chain) * 2 + c]
        if j:
            remote(source, source, shot_send.at[j - 1], shot_recv.at[j - 1], (f, chips[j])).wait_recv()
        forwards.append(remote(source, source, core_send.at[j], core_recv.at[j], sibling))
        forwards[-1].start()
    for j in range(chain):
        landing = gathered.at[lax.rem(z + chain - j, chain) * 2 + 1 - c]
        remote(landing, landing, core_send.at[j], core_recv.at[j], sibling).wait_recv()

    for p in range(TILE_DEV):
        wanted = order_ref[s * TILE_DEV + p].astype(F32)
        picked = jnp.zeros((DEPTH * rows // 8, 8, term_ref.shape[3]), F32)
        for other in range(shots):
            for a in range(aper):
                hit = gathered[other, a, DEPTH * rows :] == wanted
                value = gathered[other, a, : DEPTH * rows].reshape(picked.shape)
                picked += jnp.where(hit[None], value, 0.0)
        out_ref[p] = picked.reshape(DEPTH, rows, -1)
    for copy in sums + sends + forwards:
        copy.wait_send()


def exchange_image(freqs, shots, ids, order, terms):
    aper, _, height, tile_width = terms.shape
    rows = height // freqs
    chain = shots // 2
    smem = pl.BlockSpec(memory_space=pltpu.SMEM)
    vmem = pl.BlockSpec(memory_space=pltpu.VMEM)
    dma = pltpu.SemaphoreType.DMA
    image = pl.pallas_call(
        functools.partial(image_kernel, freqs, shots),
        in_specs=[smem, smem, vmem],
        out_specs=vmem,
        out_shape=jax.ShapeDtypeStruct((TILE_DEV, DEPTH, rows, tile_width), F32),
        scratch_shapes=[
            pltpu.VMEM((freqs - 1, aper, DEPTH, rows, tile_width), F32),
            pltpu.VMEM((shots, aper, DEPTH * rows + 8, tile_width), F32),
            dma((freqs - 1,)), dma((freqs - 1,)), dma((chain - 1,)), dma((chain - 1,)),
            dma((chain,)), dma((chain,)),
        ],
        compiler_params=pltpu.CompilerParams(
            collective_id=1, has_side_effects=True, vmem_limit_bytes=48 * 2**20
        ),
        name="exchange_image",
    )(ids, order, terms)
    return image.reshape(TILE_DEV, DEPTH, rows * tile_width)


def local(
    freqs, shots, source_field, receiver_field, angular_freq, x_correction, y_correction,
    velocity, slab_owner, apertures, tile_order,
):
    tile_ids = apertures[0]
    first_source, first_receiver, source, receiver = exchange_slabs(
        freqs, shots, slab_owner, angular_freq, velocity, source_field, receiver_field,
        x_correction, y_correction,
    )
    source, receiver, terms = last_sweep(
        angular_freq.shape[0] * freqs, tile_order.shape[0],
        tile_ids, y_correction, first_source, first_receiver, source, receiver,
    )
    return source, receiver, exchange_image(freqs, shots, tile_ids, tile_order, terms)


def solution(mesh):
    in_specs = (
        P("freq", "shot", None, None, None),
        P("freq", "shot", None, None, None),
        P("freq"),
        P("freq", None, None, None),
        P("freq", None, None, None),
        P("shot", None, None),
        P(),
        P("shot", None),
        P(),
    )
    out_specs = (
        P("freq", "shot", None, None, None),
        P("freq", "shot", None, None, None),
        P("shot", None, "freq"),
    )
    body = functools.partial(local, mesh.shape["freq"], mesh.shape["shot"])
    return jax.shard_map(body, mesh=mesh, in_specs=in_specs, out_specs=out_specs, check_vma=False)
```

```python
import functools
import math

import jax
import jax.numpy as jnp
from jax import lax
from jax.experimental import pallas as pl
from jax.experimental.pallas import tpu as pltpu
from jax.sharding import PartitionSpec as P

DEPTH = 2
TILE_DEV = 4
CHUNK = 256
LAST_CHUNK = 1024
SIN = (4.44288292, -7.3082457, 3.60635441, -0.84611287, 0.10982695)
COS = (1.4142135, -6.97885099, 5.73946116, -1.88356292, 0.31069804)
F32 = jnp.float32
BF16 = jnp.bfloat16
MESH = pl.DeviceIdType.MESH
HOP = 2
PLANE = 3
CORE = 2


def horner(coefficients, z):
    total = jnp.full_like(z, coefficients[-1])
    for coefficient in coefficients[-2::-1]:
        total = total * z + coefficient
    return total


def cos_sin(turns):
    r = turns - jnp.round(turns)
    z = r * r
    half_sin = r * horner(SIN, z)
    half_cos = horner(COS, z)
    return 1.0 - half_sin * half_sin, half_sin * half_cos


def pair_matrix(real, below_left, above_right):
    return jnp.concatenate(
        [jnp.concatenate([real, above_right], axis=1), jnp.concatenate([below_left, real], axis=1)], axis=0
    )


def x_matrix(x_ref, f):
    return pair_matrix(x_ref[f, 0], -x_ref[f, 1], x_ref[f, 1])


def y_matrix(y_ref, f):
    real = y_ref[f, 0].astype(F32).T.astype(BF16)
    imag = y_ref[f, 1].astype(F32).T.astype(BF16)
    return pair_matrix(real, imag, -imag)


def sweep_x(re, im, mx):
    rows = jnp.concatenate(
        [
            jnp.concatenate([re[:, t : t + 128], im[:, t : t + 128]], axis=1)
            for t in range(0, re.shape[1], 128)
        ],
        axis=0,
    )
    swept = (rows.astype(F32) + jnp.dot(rows, mx, preferred_element_type=F32)).astype(BF16)
    height = re.shape[0]
    return [
        jnp.concatenate([swept[t : t + height, c : c + 128] for t in range(0, swept.shape[0], height)], axis=1)
        for c in (0, 128)
    ]


def sweep_y(re, im, my):
    columns = jnp.concatenate([re, im], axis=0)
    out = columns.astype(F32) + jnp.dot(my, columns, preferred_element_type=F32)
    return out[: re.shape[0]], out[re.shape[0] :]


def last_kernel(
    freq_total, ids_ref, y_ref, source_ref, receiver_ref, first_source, first_receiver, half_source, half_receiver,
    source_out, receiver_out, term_ref, my, tiles, tile_sem,
):
    step = pl.program_id(0)
    aper = term_ref.shape[0]
    tile_width = term_ref.shape[-1]
    share = 128 // tile_width
    whole = ((first_source, first_receiver), (half_source, half_receiver))

    def loads(a):
        at = pl.ds(pl.multiple_of(ids_ref[a] // share * 128, 128), 128)
        return [
            pltpu.make_async_copy(
                whole[d][field].at[:, 0, :, :, at], tiles.at[a, d, field], tile_sem.at[a, d, field]
            )
            for d in range(DEPTH)
            for field in range(2)
        ]

    @pl.when(step == 0)
    def _():
        for a in range(aper):
            for load in loads(a):
                load.start()
        for f in range(y_ref.shape[0]):
            my[f] = y_matrix(y_ref, f)

    for f in range(source_ref.shape[0]):
        re, im = sweep_y(source_ref[f, 0, 0], source_ref[f, 0, 1], my[f])
        source_out[f, 0, 0] = re.astype(BF16)
        source_out[f, 0, 1] = im.astype(BF16)
        re, im = sweep_y(receiver_ref[f, 0, 0], receiver_ref[f, 0, 1], my[f])
        receiver_out[f, 0, 0] = re.astype(BF16)
        receiver_out[f, 0, 1] = (-im).astype(BF16)

    @pl.when(step == pl.num_programs(0) - 1)
    def _():
        for a in range(aper):
            for load in loads(a):
                load.wait()
            place = ids_ref[a] % share
            for d in range(DEPTH):
                total = jnp.zeros((term_ref.shape[2], 128), F32)
                for f in range(source_ref.shape[0]):
                    re, im = [
                        jnp.concatenate([tiles[a, d, field, f, part] for field in range(2)], axis=1)
                        for part in range(2)
                    ]
                    if d == DEPTH - 1:
                        re, im = [value.astype(BF16) for value in sweep_y(re, im, my[f])]
                    re, im = re.astype(F32), im.astype(F32)
                    total += re[:, :128] * re[:, 128:] - im[:, :128] * im[:, 128:]
                total = total * (1.0 / freq_total)
                picked = total[:, :tile_width]
                for p in range(1, share):
                    picked = jnp.where(place == p, total[:, p * tile_width : (p + 1) * tile_width], picked)
                term_ref[a, d] = picked


def last_sweep(freq_total, tile_total, ids, yc, first_source, first_receiver, source, receiver):
    count, _, _, height, width = source.shape
    aper = ids.shape[0]
    spec = pl.BlockSpec((count, 1, 2, height, LAST_CHUNK), lambda i: (0, 0, 0, 0, i))
    shape = jax.ShapeDtypeStruct(source.shape, BF16)
    term = (aper, DEPTH, height, width // tile_total)
    anywhere = pl.BlockSpec(memory_space=pl.ANY)
    return pl.pallas_call(
        functools.partial(last_kernel, freq_total),
        grid=(width // LAST_CHUNK,),
        in_specs=[
            pl.BlockSpec(memory_space=pltpu.SMEM), pl.BlockSpec(yc.shape, lambda i: (0, 0, 0, 0)),
            spec, spec, anywhere, anywhere, anywhere, anywhere,
        ],
        out_specs=[spec, spec, pl.BlockSpec(term, lambda i: (0, 0, 0, 0))],
        out_shape=[shape, shape, jax.ShapeDtypeStruct(term, F32)],
        scratch_shapes=[
            pltpu.VMEM((count, 256, 256), BF16),
            pltpu.VMEM((aper, DEPTH, 2, count, 2, height, 128), BF16),
            pltpu.SemaphoreType.DMA((aper, DEPTH, 2)),
        ],
        compiler_params=pltpu.CompilerParams(vmem_limit_bytes=60 * 2**20),
        name="last_sweep",
    )(ids, yc, source, receiver, first_source, first_receiver, source, receiver)


def greet(devices, count):
    barrier = pltpu.get_barrier_semaphore()
    for there, device in devices:
        if there is None:
            pl.semaphore_signal(barrier, inc=1, device_id=device, device_id_type=MESH)
        else:

            @pl.when(there)
            def _(device=device):
                pl.semaphore_signal(barrier, inc=1, device_id=device, device_id_type=MESH)

    pl.semaphore_wait(barrier, count)


def remote(src, dst, send, recv, device):
    return pltpu.make_async_remote_copy(
        src_ref=src, dst_ref=dst, send_sem=send, recv_sem=recv, device_id=device, device_id_type=MESH
    )


def slab_kernel(
    freqs, shots, owner_ref, freq_ref, velocity_ref, source_ref, receiver_ref, x_ref, y_ref,
    source_first, receiver_first, source_out, receiver_out,
    slabs, own_part, sibling_part, mine, up_out, up_in, down_out, down_in, fields, stage, mx, my,
    pair_sem, up_sem, down_sem, plane_send, plane_recv, core_send, core_recv, in_sem, out_sem,
):
    f = lax.axis_index("freq")
    s = lax.axis_index("shot")
    chain = shots // 2
    z = s // 2
    c = s % 2
    rows, width = slabs.shape[2], slabs.shape[3]
    chunks = width // CHUNK
    sibling = (f, z * 2 + 1 - c)
    above = (f, jnp.minimum(s + 2, shots - 2 + c))
    below = (f, jnp.maximum(s - 2, c))
    own = f * 2 + c
    field_refs = (source_ref, receiver_ref)
    out_refs = (source_first, receiver_first, source_out, receiver_out)
    count, height = source_ref.shape[0], source_ref.shape[3]
    loads = [
        pltpu.make_async_copy(field_refs[i].at[:, 0], fields.at[i], in_sem.at[i]) for i in range(2)
    ]
    others = [(lax.rem(f + j, freqs), s) for j in range(1, freqs)]
    has_below = z > 0
    has_above = z < chain - 1
    greet(
        [(None, sibling)] + [(None, o) for o in others] + [(has_above, above), (has_below, below)],
        freqs + has_above.astype(jnp.int32) + has_below.astype(jnp.int32),
    )

    def row_slice(index):
        return pl.ds(pl.multiple_of(index * rows, 8), rows)

    pair = remote(
        velocity_ref.at[0, row_slice(f * 2 + 1 - c)], sibling_part, pair_sem.at[0], pair_sem.at[1], sibling
    )
    pair.start()
    own_load = pltpu.make_async_copy(velocity_ref.at[0, row_slice(own)], own_part, in_sem.at[2])
    own_load.start()
    for load in loads:
        load.start()
    for i in range(count):
        mx[i] = x_matrix(x_ref, i)
        my[i] = y_matrix(y_ref, i)

    @pl.when(z == 0)
    def _():
        up_in[...] = jnp.zeros_like(up_in)

    @pl.when(z == chain - 1)
    def _():
        down_in[...] = jnp.zeros_like(down_in)

    own_load.wait()
    pair.wait_recv()
    here = own_part[...]
    there = sibling_part[...]
    for d in range(DEPTH):
        held = jnp.where(owner_ref[d] == s, here, jnp.zeros_like(here))
        mine[d] = jnp.where(owner_ref[d] == z * 2 + 1 - c, there, held)

    def at(k):
        return pl.ds(pl.multiple_of(k * CHUNK, CHUNK), CHUNK)

    def up_copy(k):
        return remote(
            up_out.at[:, :, at(k)], up_in.at[:, :, at(k)], up_sem.at[0, k], up_sem.at[1, k], above
        )

    def down_copy(k):
        return remote(
            down_out.at[:, :, at(k)], down_in.at[:, :, at(k)], down_sem.at[0, k], down_sem.at[1, k], below
        )

    def plane_copy(j, k):
        place = slabs.at[:, own, :, at(k)]
        return remote(place, place, plane_send.at[j - 1, k], plane_recv.at[j - 1, k], others[j - 1])

    def core_copy(j, k):
        place = slabs.at[:, lax.rem(f + freqs - j, freqs) * 2 + c, :, at(k)]
        return remote(place, place, core_send.at[j, k], core_recv.at[j, k], sibling)

    def arrived(j, k):
        place = slabs.at[:, lax.rem(f + freqs - j, freqs) * 2 + c, :, at(k)]
        return remote(place, place, plane_send.at[j - 1, k], plane_recv.at[j - 1, k], others[j - 1])

    def core_arrived(j, k):
        place = slabs.at[:, lax.rem(f + freqs - j, freqs) * 2 + 1 - c, :, at(k)]
        return remote(place, place, core_send.at[j, k], core_recv.at[j, k], sibling)

    def go_up(k):
        @pl.when(has_below)
        def _():
            up_copy(k).wait_recv()

        @pl.when(has_above)
        def _():
            up_out[:, :, at(k)] = up_in[:, :, at(k)] + mine[:, :, at(k)]
            up_copy(k).start()

    def go_down(k):
        @pl.when(has_above)
        def _():
            down_copy(k).wait_recv()

        @pl.when(has_below)
        def _():
            down_out[:, :, at(k)] = down_in[:, :, at(k)] + mine[:, :, at(k)]
            down_copy(k).start()

    z_lag = HOP * (chain - 1)
    plane_lag = z_lag + PLANE
    core_lag = plane_lag + CORE

    def out_copy(i, k):
        held = fields if i < 2 else stage
        return pltpu.make_async_copy(
            held.at[i % 2, :, :, :, at(k)], out_refs[i].at[:, 0, :, :, at(k)], out_sem.at[i, k]
        )

    def compute(k):
        for i in range(count):
            scale = freq_ref[i] * (0.5 / math.pi)
            cosine, sine = cos_sin(slabs[0, :, :, at(k)].reshape(height, CHUNK) * scale)
            sre, sim, rre, rim = [
                fields[field, i, part, :, at(k)].astype(F32) for field in range(2) for part in range(2)
            ]
            re = jnp.concatenate([sre * cosine - sim * sine, rre * cosine + rim * sine], axis=1)
            im = jnp.concatenate([sre * sine + sim * cosine, rre * sine - rim * cosine], axis=1)
            re, im = sweep_y(*sweep_x(re.astype(BF16), im.astype(BF16), mx[i]), my[i])
            re, im = re.astype(BF16), im.astype(BF16)
            for field in range(2):
                fields[field, i, 0, :, at(k)] = re[:, field * CHUNK : (field + 1) * CHUNK]
                fields[field, i, 1, :, at(k)] = im[:, field * CHUNK : (field + 1) * CHUNK]
            cosine, sine = cos_sin(slabs[1, :, :, at(k)].reshape(height, CHUNK) * scale)
            cosine = jnp.concatenate([cosine, cosine], axis=1)
            sine = jnp.concatenate([sine, sine], axis=1)
            re, im = re.astype(F32), im.astype(F32)
            re, im = sweep_x(
                (re * cosine - im * sine).astype(BF16), (re * sine + im * cosine).astype(BF16), mx[i]
            )
            for field in range(2):
                stage[field, i, 0, :, at(k)] = re[:, field * CHUNK : (field + 1) * CHUNK]
                stage[field, i, 1, :, at(k)] = im[:, field * CHUNK : (field + 1) * CHUNK]

    def step(i, carry):
        for first, go in ((HOP * z, go_up), (HOP * (chain - 1 - z), go_down)):

            @pl.when(jnp.logical_and(i >= first, i < chunks + first))
            def _(first=first, go=go):
                go(i - first)

        @pl.when(jnp.logical_and(i >= z_lag, i < chunks + z_lag))
        def _():
            k = i - z_lag
            slabs[:, own, :, at(k)] = up_in[:, :, at(k)] + mine[:, :, at(k)] + down_in[:, :, at(k)]
            for j in range(1, freqs):
                plane_copy(j, k).start()
            core_copy(0, k).start()

        @pl.when(jnp.logical_and(i >= plane_lag, i < chunks + plane_lag))
        def _():
            k = i - plane_lag
            for j in range(1, freqs):
                arrived(j, k).wait_recv()
                core_copy(j, k).start()

        @pl.when(i == core_lag)
        def _():
            for load in loads:
                load.wait()

        @pl.when(i >= core_lag)
        def _():
            k = i - core_lag
            for j in range(freqs):
                core_arrived(j, k).wait_recv()
            compute(k)
            for out in range(4):
                out_copy(out, k).start()

        return carry

    lax.fori_loop(0, chunks + core_lag, step, 0)
    pair.wait_send()

    def drain(k, carry):
        @pl.when(has_above)
        def _():
            up_copy(k).wait_send()

        @pl.when(has_below)
        def _():
            down_copy(k).wait_send()

        for j in range(1, freqs):
            plane_copy(j, k).wait_send()
        for j in range(freqs):
            core_copy(j, k).wait_send()
        for out in range(4):
            out_copy(out, k).wait()
        return carry

    lax.fori_loop(0, chunks, drain, 0)


def exchange_slabs(freqs, shots, owners, freq, velocity, source, receiver, xc, yc):
    _, height, width = velocity.shape
    count = source.shape[0]
    rows = height // (2 * freqs)
    chunks = width // CHUNK
    vmem = pl.BlockSpec(memory_space=pltpu.VMEM)
    smem = pl.BlockSpec(memory_space=pltpu.SMEM)
    anywhere = pl.BlockSpec(memory_space=pl.ANY)
    strip = pltpu.VMEM((DEPTH, rows, width), F32)
    field = pltpu.VMEM((2, count, 2, height, width), BF16)
    matrix = pltpu.VMEM((count, 256, 256), BF16)
    dma = pltpu.SemaphoreType.DMA
    shape = jax.ShapeDtypeStruct(source.shape, BF16)
    return pl.pallas_call(
        functools.partial(slab_kernel, freqs, shots),
        in_specs=[smem, smem, anywhere, anywhere, anywhere, vmem, vmem],
        out_specs=[anywhere] * 4,
        out_shape=[shape] * 4,
        scratch_shapes=[
            pltpu.VMEM((DEPTH, 2 * freqs, rows, width), F32),
            pltpu.VMEM((rows, width), F32),
            pltpu.VMEM((rows, width), F32),
            strip, strip, strip, strip, strip, field, field, matrix, matrix,
            dma((2,)), dma((2, chunks)), dma((2, chunks)),
            dma((freqs - 1, chunks)), dma((freqs - 1, chunks)),
            dma((freqs, chunks)), dma((freqs, chunks)), dma((3,)), dma((4, chunks)),
        ],
        compiler_params=pltpu.CompilerParams(
            collective_id=0, has_side_effects=True, vmem_limit_bytes=60 * 2**20
        ),
        name="slabs_and_sweeps",
    )(owners, freq, velocity, source, receiver, xc, yc)


def image_kernel(
    freqs, shots, ids_ref, order_ref, term_ref, out_ref,
    landed, gathered, sum_send, sum_recv, shot_send, shot_recv, core_send, core_recv,
):
    f = lax.axis_index("freq")
    s = lax.axis_index("shot")
    chain = shots // 2
    z = s // 2
    c = s % 2
    aper = term_ref.shape[0]
    rows = out_ref.shape[2]
    sibling = (f, z * 2 + 1 - c)
    others = [(lax.rem(f + j, freqs), s) for j in range(1, freqs)]
    chips = [lax.rem(z + j, chain) * 2 + c for j in range(chain)]
    greet(
        [(None, sibling)] + [(None, o) for o in others] + [(None, (f, chip)) for chip in chips[1:]],
        freqs + chain - 1,
    )

    def row_slice(index):
        return pl.ds(pl.multiple_of(index * rows, 8), rows)

    sums = [
        remote(
            term_ref.at[:, :, row_slice(others[j - 1][0])], landed.at[j - 1],
            sum_send.at[j - 1], sum_recv.at[j - 1], others[j - 1],
        )
        for j in range(1, freqs)
    ]
    for copy in sums:
        copy.start()
    for a in range(aper):
        gathered[s, a, DEPTH * rows :] = jnp.full((8, term_ref.shape[3]), ids_ref[a].astype(F32))
    total = term_ref[:, :, row_slice(f)]
    for j in range(1, freqs):
        sums[j - 1].wait_recv()
        total = total + landed[j - 1]
    gathered[s, :, : DEPTH * rows] = total.reshape(aper, DEPTH * rows, -1)

    place = gathered.at[s]
    sends = [
        remote(place, place, shot_send.at[j - 1], shot_recv.at[j - 1], (f, chips[j])) for j in range(1, chain)
    ]
    for copy in sends:
        copy.start()
    forwards = []
    for j in range(chain):
        source = gathered.at[lax.rem(z + chain - j, chain) * 2 + c]
        if j:
            remote(source, source, shot_send.at[j - 1], shot_recv.at[j - 1], (f, chips[j])).wait_recv()
        forwards.append(remote(source, source, core_send.at[j], core_recv.at[j], sibling))
        forwards[-1].start()
    for j in range(chain):
        landing = gathered.at[lax.rem(z + chain - j, chain) * 2 + 1 - c]
        remote(landing, landing, core_send.at[j], core_recv.at[j], sibling).wait_recv()

    for p in range(TILE_DEV):
        wanted = order_ref[s * TILE_DEV + p].astype(F32)
        picked = jnp.zeros((DEPTH * rows // 8, 8, term_ref.shape[3]), F32)
        for other in range(shots):
            for a in range(aper):
                hit = gathered[other, a, DEPTH * rows :] == wanted
                value = gathered[other, a, : DEPTH * rows].reshape(picked.shape)
                picked += jnp.where(hit[None], value, 0.0)
        out_ref[p] = picked.reshape(DEPTH, rows, -1)
    for copy in sums + sends + forwards:
        copy.wait_send()


def exchange_image(freqs, shots, ids, order, terms):
    aper, _, height, tile_width = terms.shape
    rows = height // freqs
    chain = shots // 2
    smem = pl.BlockSpec(memory_space=pltpu.SMEM)
    vmem = pl.BlockSpec(memory_space=pltpu.VMEM)
    dma = pltpu.SemaphoreType.DMA
    image = pl.pallas_call(
        functools.partial(image_kernel, freqs, shots),
        in_specs=[smem, smem, vmem],
        out_specs=vmem,
        out_shape=jax.ShapeDtypeStruct((TILE_DEV, DEPTH, rows, tile_width), F32),
        scratch_shapes=[
            pltpu.VMEM((freqs - 1, aper, DEPTH, rows, tile_width), F32),
            pltpu.VMEM((shots, aper, DEPTH * rows + 8, tile_width), F32),
            dma((freqs - 1,)), dma((freqs - 1,)), dma((chain - 1,)), dma((chain - 1,)),
            dma((chain,)), dma((chain,)),
        ],
        compiler_params=pltpu.CompilerParams(
            collective_id=1, has_side_effects=True, vmem_limit_bytes=60 * 2**20
        ),
        name="exchange_image",
    )(ids, order, terms)
    return image.reshape(TILE_DEV, DEPTH, rows * tile_width)


def local(
    freqs, shots, source_field, receiver_field, angular_freq, x_correction, y_correction,
    velocity, slab_owner, apertures, tile_order,
):
    tile_ids = apertures[0]
    first_source, first_receiver, source, receiver = exchange_slabs(
        freqs, shots, slab_owner, angular_freq, velocity, source_field, receiver_field,
        x_correction, y_correction,
    )
    source, receiver, terms = last_sweep(
        angular_freq.shape[0] * freqs, tile_order.shape[0],
        tile_ids, y_correction, first_source, first_receiver, source, receiver,
    )
    return source, receiver, exchange_image(freqs, shots, tile_ids, tile_order, terms)


def solution(mesh):
    in_specs = (
        P("freq", "shot", None, None, None),
        P("freq", "shot", None, None, None),
        P("freq"),
        P("freq", None, None, None),
        P("freq", None, None, None),
        P("shot", None, None),
        P(),
        P("shot", None),
        P(),
    )
    out_specs = (
        P("freq", "shot", None, None, None),
        P("freq", "shot", None, None, None),
        P("shot", None, "freq"),
    )
    body = functools.partial(local, mesh.shape["freq"], mesh.shape["shot"])
    return jax.shard_map(body, mesh=mesh, in_specs=in_specs, out_specs=out_specs, check_vma=False)
```

```python
import functools
import math

import jax
import jax.numpy as jnp
from jax import lax
from jax.experimental import pallas as pl
from jax.experimental.pallas import tpu as pltpu
from jax.sharding import PartitionSpec as P

DEPTH = 2
TILE_DEV = 4
CHUNK = 512
LAST_CHUNK = 1024
SIN = (4.44288292, -7.3082457, 3.60635441, -0.84611287, 0.10982695)
COS = (1.4142135, -6.97885099, 5.73946116, -1.88356292, 0.31069804)
F32 = jnp.float32
BF16 = jnp.bfloat16
MESH = pl.DeviceIdType.MESH
HOP = 2
PLANE = 2
CORE = 1


def horner(coefficients, z):
    total = jnp.full_like(z, coefficients[-1])
    for coefficient in coefficients[-2::-1]:
        total = total * z + coefficient
    return total


def cos_sin(turns):
    r = turns - jnp.round(turns)
    z = r * r
    half_sin = r * horner(SIN, z)
    half_cos = horner(COS, z)
    return 1.0 - half_sin * half_sin, half_sin * half_cos


def pair_matrix(real, below_left, above_right):
    return jnp.concatenate(
        [jnp.concatenate([real, above_right], axis=1), jnp.concatenate([below_left, real], axis=1)], axis=0
    )


def x_matrix(x_ref, f):
    return pair_matrix(x_ref[f, 0], -x_ref[f, 1], x_ref[f, 1])


def y_matrix(y_ref, f):
    real = y_ref[f, 0].astype(F32).T.astype(BF16)
    imag = y_ref[f, 1].astype(F32).T.astype(BF16)
    return pair_matrix(real, imag, -imag)


def sweep_x(re, im, mx):
    rows = jnp.concatenate(
        [
            jnp.concatenate([re[:, t : t + 128], im[:, t : t + 128]], axis=1)
            for t in range(0, re.shape[1], 128)
        ],
        axis=0,
    )
    swept = (rows.astype(F32) + jnp.dot(rows, mx, preferred_element_type=F32)).astype(BF16)
    height = re.shape[0]
    return [
        jnp.concatenate([swept[t : t + height, c : c + 128] for t in range(0, swept.shape[0], height)], axis=1)
        for c in (0, 128)
    ]


def sweep_y(re, im, my):
    columns = jnp.concatenate([re, im], axis=0)
    out = columns.astype(F32) + jnp.dot(my, columns, preferred_element_type=F32)
    return out[: re.shape[0]], out[re.shape[0] :]


def last_kernel(
    freq_total, ids_ref, x_ref, y_ref, source_ref, receiver_ref, first_source, first_receiver, half_source, half_receiver,
    source_out, receiver_out, term_ref, mx, my, tiles, tile_sem,
):
    step = pl.program_id(0)
    aper = term_ref.shape[0]
    tile_width = term_ref.shape[-1]
    share = 128 // tile_width
    whole = ((first_source, first_receiver), (half_source, half_receiver))

    def loads(a):
        at = pl.ds(pl.multiple_of(ids_ref[a] // share * 128, 128), 128)
        return [
            pltpu.make_async_copy(
                whole[d][field].at[:, 0, :, :, at], tiles.at[a, d, field], tile_sem.at[a, d, field]
            )
            for d in range(DEPTH)
            for field in range(2)
        ]

    @pl.when(step == 0)
    def _():
        for a in range(aper):
            for load in loads(a):
                load.start()
        for f in range(y_ref.shape[0]):
            mx[f] = x_matrix(x_ref, f)
            my[f] = y_matrix(y_ref, f)

    for f in range(source_ref.shape[0]):
        re, im = sweep_y(*sweep_x(source_ref[f, 0, 0], source_ref[f, 0, 1], mx[f]), my[f])
        source_out[f, 0, 0] = re.astype(BF16)
        source_out[f, 0, 1] = im.astype(BF16)
        re, im = sweep_y(*sweep_x(receiver_ref[f, 0, 0], receiver_ref[f, 0, 1], mx[f]), my[f])
        receiver_out[f, 0, 0] = re.astype(BF16)
        receiver_out[f, 0, 1] = (-im).astype(BF16)

    @pl.when(step == pl.num_programs(0) - 1)
    def _():
        for a in range(aper):
            for load in loads(a):
                load.wait()
            place = ids_ref[a] % share
            for d in range(DEPTH):
                total = jnp.zeros((term_ref.shape[2], 128), F32)
                for f in range(source_ref.shape[0]):
                    re, im = [
                        jnp.concatenate([tiles[a, d, field, f, part] for field in range(2)], axis=1)
                        for part in range(2)
                    ]
                    if d == DEPTH - 1:
                        re, im = [value.astype(BF16) for value in sweep_y(*sweep_x(re, im, mx[f]), my[f])]
                    re, im = re.astype(F32), im.astype(F32)
                    total += re[:, :128] * re[:, 128:] - im[:, :128] * im[:, 128:]
                total = total * (1.0 / freq_total)
                picked = total[:, :tile_width]
                for p in range(1, share):
                    picked = jnp.where(place == p, total[:, p * tile_width : (p + 1) * tile_width], picked)
                term_ref[a, d] = picked


def last_sweep(freq_total, tile_total, ids, xc, yc, first_source, first_receiver, source, receiver):
    count, _, _, height, width = source.shape
    aper = ids.shape[0]
    spec = pl.BlockSpec((count, 1, 2, height, LAST_CHUNK), lambda i: (0, 0, 0, 0, i))
    shape = jax.ShapeDtypeStruct(source.shape, BF16)
    term = (aper, DEPTH, height, width // tile_total)
    anywhere = pl.BlockSpec(memory_space=pl.ANY)
    return pl.pallas_call(
        functools.partial(last_kernel, freq_total),
        grid=(width // LAST_CHUNK,),
        in_specs=[
            pl.BlockSpec(memory_space=pltpu.SMEM),
            pl.BlockSpec(xc.shape, lambda i: (0, 0, 0, 0)), pl.BlockSpec(yc.shape, lambda i: (0, 0, 0, 0)),
            spec, spec, anywhere, anywhere, anywhere, anywhere,
        ],
        out_specs=[spec, spec, pl.BlockSpec(term, lambda i: (0, 0, 0, 0))],
        out_shape=[shape, shape, jax.ShapeDtypeStruct(term, F32)],
        scratch_shapes=[
            pltpu.VMEM((count, 256, 256), BF16),
            pltpu.VMEM((count, 256, 256), BF16),
            pltpu.VMEM((aper, DEPTH, 2, count, 2, height, 128), BF16),
            pltpu.SemaphoreType.DMA((aper, DEPTH, 2)),
        ],
        compiler_params=pltpu.CompilerParams(vmem_limit_bytes=60 * 2**20),
        name="last_sweeps",
    )(ids, xc, yc, source, receiver, first_source, first_receiver, source, receiver)


def greet(devices, count):
    barrier = pltpu.get_barrier_semaphore()
    for there, device in devices:
        if there is None:
            pl.semaphore_signal(barrier, inc=1, device_id=device, device_id_type=MESH)
        else:

            @pl.when(there)
            def _(device=device):
                pl.semaphore_signal(barrier, inc=1, device_id=device, device_id_type=MESH)

    pl.semaphore_wait(barrier, count)


def remote(src, dst, send, recv, device):
    return pltpu.make_async_remote_copy(
        src_ref=src, dst_ref=dst, send_sem=send, recv_sem=recv, device_id=device, device_id_type=MESH
    )


def slab_kernel(
    freqs, shots, owner_ref, freq_ref, velocity_ref, source_ref, receiver_ref, x_ref, y_ref,
    source_first, receiver_first, source_out, receiver_out,
    slabs, own_part, sibling_part, mine, up_out, up_in, down_out, down_in, fields, stage, mx, my,
    pair_sem, up_sem, down_sem, plane_send, plane_recv, core_send, core_recv, in_sem, out_sem,
):
    f = lax.axis_index("freq")
    s = lax.axis_index("shot")
    chain = shots // 2
    z = s // 2
    c = s % 2
    rows, width = slabs.shape[2], slabs.shape[3]
    chunks = width // CHUNK
    sibling = (f, z * 2 + 1 - c)
    above = (f, jnp.minimum(s + 2, shots - 2 + c))
    below = (f, jnp.maximum(s - 2, c))
    own = f * 2 + c
    field_refs = (source_ref, receiver_ref)
    out_refs = (source_first, receiver_first, source_out, receiver_out)
    count, height = source_ref.shape[0], source_ref.shape[3]
    loads = [
        pltpu.make_async_copy(field_refs[i].at[:, 0], fields.at[i], in_sem.at[i]) for i in range(2)
    ]
    others = [(lax.rem(f + j, freqs), s) for j in range(1, freqs)]
    has_below = z > 0
    has_above = z < chain - 1
    greet(
        [(None, sibling)] + [(None, o) for o in others] + [(has_above, above), (has_below, below)],
        freqs + has_above.astype(jnp.int32) + has_below.astype(jnp.int32),
    )

    def row_slice(index):
        return pl.ds(pl.multiple_of(index * rows, 8), rows)

    pair = remote(
        velocity_ref.at[0, row_slice(f * 2 + 1 - c)], sibling_part, pair_sem.at[0], pair_sem.at[1], sibling
    )
    pair.start()
    own_load = pltpu.make_async_copy(velocity_ref.at[0, row_slice(own)], own_part, in_sem.at[2])
    own_load.start()
    for load in loads:
        load.start()
    for i in range(count):
        mx[i] = x_matrix(x_ref, i)
        my[i] = y_matrix(y_ref, i)

    @pl.when(z == 0)
    def _():
        up_in[...] = jnp.zeros_like(up_in)

    @pl.when(z == chain - 1)
    def _():
        down_in[...] = jnp.zeros_like(down_in)

    own_load.wait()
    pair.wait_recv()
    here = own_part[...]
    there = sibling_part[...]
    for d in range(DEPTH):
        held = jnp.where(owner_ref[d] == s, here, jnp.zeros_like(here))
        mine[d] = jnp.where(owner_ref[d] == z * 2 + 1 - c, there, held)

    def at(k):
        return pl.ds(pl.multiple_of(k * CHUNK, CHUNK), CHUNK)

    def up_copy(k):
        return remote(
            up_out.at[:, :, at(k)], up_in.at[:, :, at(k)], up_sem.at[0, k], up_sem.at[1, k], above
        )

    def down_copy(k):
        return remote(
            down_out.at[:, :, at(k)], down_in.at[:, :, at(k)], down_sem.at[0, k], down_sem.at[1, k], below
        )

    def plane_copy(j, k):
        place = slabs.at[:, own, :, at(k)]
        return remote(place, place, plane_send.at[j - 1, k], plane_recv.at[j - 1, k], others[j - 1])

    def core_copy(j, k):
        place = slabs.at[:, lax.rem(f + freqs - j, freqs) * 2 + c, :, at(k)]
        return remote(place, place, core_send.at[j, k], core_recv.at[j, k], sibling)

    def arrived(j, k):
        place = slabs.at[:, lax.rem(f + freqs - j, freqs) * 2 + c, :, at(k)]
        return remote(place, place, plane_send.at[j - 1, k], plane_recv.at[j - 1, k], others[j - 1])

    def core_arrived(j, k):
        place = slabs.at[:, lax.rem(f + freqs - j, freqs) * 2 + 1 - c, :, at(k)]
        return remote(place, place, core_send.at[j, k], core_recv.at[j, k], sibling)

    def go_up(k):
        @pl.when(has_below)
        def _():
            up_copy(k).wait_recv()

        @pl.when(has_above)
        def _():
            up_out[:, :, at(k)] = up_in[:, :, at(k)] + mine[:, :, at(k)]
            up_copy(k).start()

    def go_down(k):
        @pl.when(has_above)
        def _():
            down_copy(k).wait_recv()

        @pl.when(has_below)
        def _():
            down_out[:, :, at(k)] = down_in[:, :, at(k)] + mine[:, :, at(k)]
            down_copy(k).start()

    z_lag = HOP * (chain - 1)
    plane_lag = z_lag + PLANE
    core_lag = plane_lag + CORE

    def out_copy(i, k):
        held = fields if i < 2 else stage
        return pltpu.make_async_copy(
            held.at[i % 2, :, :, :, at(k)], out_refs[i].at[:, 0, :, :, at(k)], out_sem.at[i, k]
        )

    def compute(k):
        for i in range(count):
            scale = freq_ref[i] * (0.5 / math.pi)
            cosine, sine = cos_sin(slabs[0, :, :, at(k)].reshape(height, CHUNK) * scale)
            sre, sim, rre, rim = [
                fields[field, i, part, :, at(k)].astype(F32) for field in range(2) for part in range(2)
            ]
            re = jnp.concatenate([sre * cosine - sim * sine, rre * cosine + rim * sine], axis=1)
            im = jnp.concatenate([sre * sine + sim * cosine, rre * sine - rim * cosine], axis=1)
            re, im = sweep_y(*sweep_x(re.astype(BF16), im.astype(BF16), mx[i]), my[i])
            re, im = re.astype(BF16), im.astype(BF16)
            for field in range(2):
                fields[field, i, 0, :, at(k)] = re[:, field * CHUNK : (field + 1) * CHUNK]
                fields[field, i, 1, :, at(k)] = im[:, field * CHUNK : (field + 1) * CHUNK]
            cosine, sine = cos_sin(slabs[1, :, :, at(k)].reshape(height, CHUNK) * scale)
            cosine = jnp.concatenate([cosine, cosine], axis=1)
            sine = jnp.concatenate([sine, sine], axis=1)
            re, im = re.astype(F32), im.astype(F32)
            re, im = (re * cosine - im * sine).astype(BF16), (re * sine + im * cosine).astype(BF16)
            for field in range(2):
                stage[field, i, 0, :, at(k)] = re[:, field * CHUNK : (field + 1) * CHUNK]
                stage[field, i, 1, :, at(k)] = im[:, field * CHUNK : (field + 1) * CHUNK]

    def step(i, carry):
        for first, go in ((HOP * z, go_up), (HOP * (chain - 1 - z), go_down)):

            @pl.when(jnp.logical_and(i >= first, i < chunks + first))
            def _(first=first, go=go):
                go(i - first)

        @pl.when(jnp.logical_and(i >= z_lag, i < chunks + z_lag))
        def _():
            k = i - z_lag
            slabs[:, own, :, at(k)] = up_in[:, :, at(k)] + mine[:, :, at(k)] + down_in[:, :, at(k)]
            for j in range(1, freqs):
                plane_copy(j, k).start()
            core_copy(0, k).start()

        @pl.when(jnp.logical_and(i >= plane_lag, i < chunks + plane_lag))
        def _():
            k = i - plane_lag
            for j in range(1, freqs):
                arrived(j, k).wait_recv()
                core_copy(j, k).start()

        @pl.when(i == core_lag)
        def _():
            for load in loads:
                load.wait()

        @pl.when(i >= core_lag)
        def _():
            k = i - core_lag
            for j in range(freqs):
                core_arrived(j, k).wait_recv()
            compute(k)
            for out in range(4):
                out_copy(out, k).start()

        return carry

    lax.fori_loop(0, chunks + core_lag, step, 0)
    pair.wait_send()

    def drain(k, carry):
        @pl.when(has_above)
        def _():
            up_copy(k).wait_send()

        @pl.when(has_below)
        def _():
            down_copy(k).wait_send()

        for j in range(1, freqs):
            plane_copy(j, k).wait_send()
        for j in range(freqs):
            core_copy(j, k).wait_send()
        for out in range(4):
            out_copy(out, k).wait()
        return carry

    lax.fori_loop(0, chunks, drain, 0)


def exchange_slabs(freqs, shots, owners, freq, velocity, source, receiver, xc, yc):
    _, height, width = velocity.shape
    count = source.shape[0]
    rows = height // (2 * freqs)
    chunks = width // CHUNK
    vmem = pl.BlockSpec(memory_space=pltpu.VMEM)
    smem = pl.BlockSpec(memory_space=pltpu.SMEM)
    anywhere = pl.BlockSpec(memory_space=pl.ANY)
    strip = pltpu.VMEM((DEPTH, rows, width), F32)
    field = pltpu.VMEM((2, count, 2, height, width), BF16)
    matrix = pltpu.VMEM((count, 256, 256), BF16)
    dma = pltpu.SemaphoreType.DMA
    shape = jax.ShapeDtypeStruct(source.shape, BF16)
    return pl.pallas_call(
        functools.partial(slab_kernel, freqs, shots),
        in_specs=[smem, smem, anywhere, anywhere, anywhere, vmem, vmem],
        out_specs=[anywhere] * 4,
        out_shape=[shape] * 4,
        scratch_shapes=[
            pltpu.VMEM((DEPTH, 2 * freqs, rows, width), F32),
            pltpu.VMEM((rows, width), F32),
            pltpu.VMEM((rows, width), F32),
            strip, strip, strip, strip, strip, field, field, matrix, matrix,
            dma((2,)), dma((2, chunks)), dma((2, chunks)),
            dma((freqs - 1, chunks)), dma((freqs - 1, chunks)),
            dma((freqs, chunks)), dma((freqs, chunks)), dma((3,)), dma((4, chunks)),
        ],
        compiler_params=pltpu.CompilerParams(
            collective_id=0, has_side_effects=True, vmem_limit_bytes=60 * 2**20
        ),
        name="slabs_and_sweeps",
    )(owners, freq, velocity, source, receiver, xc, yc)


def image_kernel(
    freqs, shots, ids_ref, order_ref, term_ref, out_ref,
    landed, gathered, sum_send, sum_recv, shot_send, shot_recv, core_send, core_recv,
):
    f = lax.axis_index("freq")
    s = lax.axis_index("shot")
    chain = shots // 2
    z = s // 2
    c = s % 2
    aper = term_ref.shape[0]
    rows = out_ref.shape[2]
    sibling = (f, z * 2 + 1 - c)
    others = [(lax.rem(f + j, freqs), s) for j in range(1, freqs)]
    chips = [lax.rem(z + j, chain) * 2 + c for j in range(chain)]
    greet(
        [(None, sibling)] + [(None, o) for o in others] + [(None, (f, chip)) for chip in chips[1:]],
        freqs + chain - 1,
    )

    def row_slice(index):
        return pl.ds(pl.multiple_of(index * rows, 8), rows)

    sums = [
        remote(
            term_ref.at[:, :, row_slice(others[j - 1][0])], landed.at[j - 1],
            sum_send.at[j - 1], sum_recv.at[j - 1], others[j - 1],
        )
        for j in range(1, freqs)
    ]
    for copy in sums:
        copy.start()
    for a in range(aper):
        gathered[s, a, DEPTH * rows :] = jnp.full((8, term_ref.shape[3]), ids_ref[a].astype(F32))
    total = term_ref[:, :, row_slice(f)]
    for j in range(1, freqs):
        sums[j - 1].wait_recv()
        total = total + landed[j - 1]
    gathered[s, :, : DEPTH * rows] = total.reshape(aper, DEPTH * rows, -1)

    place = gathered.at[s]
    sends = [
        remote(place, place, shot_send.at[j - 1], shot_recv.at[j - 1], (f, chips[j])) for j in range(1, chain)
    ]
    for copy in sends:
        copy.start()
    forwards = []
    for j in range(chain):
        source = gathered.at[lax.rem(z + chain - j, chain) * 2 + c]
        if j:
            remote(source, source, shot_send.at[j - 1], shot_recv.at[j - 1], (f, chips[j])).wait_recv()
        forwards.append(remote(source, source, core_send.at[j], core_recv.at[j], sibling))
        forwards[-1].start()
    for j in range(chain):
        landing = gathered.at[lax.rem(z + chain - j, chain) * 2 + 1 - c]
        remote(landing, landing, core_send.at[j], core_recv.at[j], sibling).wait_recv()

    for p in range(TILE_DEV):
        wanted = order_ref[s * TILE_DEV + p].astype(F32)
        picked = jnp.zeros((DEPTH * rows // 8, 8, term_ref.shape[3]), F32)
        for other in range(shots):
            for a in range(aper):
                hit = gathered[other, a, DEPTH * rows :] == wanted
                value = gathered[other, a, : DEPTH * rows].reshape(picked.shape)
                picked += jnp.where(hit[None], value, 0.0)
        out_ref[p] = picked.reshape(DEPTH, rows, -1)
    for copy in sums + sends + forwards:
        copy.wait_send()


def exchange_image(freqs, shots, ids, order, terms):
    aper, _, height, tile_width = terms.shape
    rows = height // freqs
    chain = shots // 2
    smem = pl.BlockSpec(memory_space=pltpu.SMEM)
    vmem = pl.BlockSpec(memory_space=pltpu.VMEM)
    dma = pltpu.SemaphoreType.DMA
    image = pl.pallas_call(
        functools.partial(image_kernel, freqs, shots),
        in_specs=[smem, smem, vmem],
        out_specs=vmem,
        out_shape=jax.ShapeDtypeStruct((TILE_DEV, DEPTH, rows, tile_width), F32),
        scratch_shapes=[
            pltpu.VMEM((freqs - 1, aper, DEPTH, rows, tile_width), F32),
            pltpu.VMEM((shots, aper, DEPTH * rows + 8, tile_width), F32),
            dma((freqs - 1,)), dma((freqs - 1,)), dma((chain - 1,)), dma((chain - 1,)),
            dma((chain,)), dma((chain,)),
        ],
        compiler_params=pltpu.CompilerParams(
            collective_id=1, has_side_effects=True, vmem_limit_bytes=60 * 2**20
        ),
        name="exchange_image",
    )(ids, order, terms)
    return image.reshape(TILE_DEV, DEPTH, rows * tile_width)


def local(
    freqs, shots, source_field, receiver_field, angular_freq, x_correction, y_correction,
    velocity, slab_owner, apertures, tile_order,
):
    tile_ids = apertures[0]
    first_source, first_receiver, source, receiver = exchange_slabs(
        freqs, shots, slab_owner, angular_freq, velocity, source_field, receiver_field,
        x_correction, y_correction,
    )
    source, receiver, terms = last_sweep(
        angular_freq.shape[0] * freqs, tile_order.shape[0],
        tile_ids, x_correction, y_correction, first_source, first_receiver, source, receiver,
    )
    return source, receiver, exchange_image(freqs, shots, tile_ids, tile_order, terms)


def solution(mesh):
    in_specs = (
        P("freq", "shot", None, None, None),
        P("freq", "shot", None, None, None),
        P("freq"),
        P("freq", None, None, None),
        P("freq", None, None, None),
        P("shot", None, None),
        P(),
        P("shot", None),
        P(),
    )
    out_specs = (
        P("freq", "shot", None, None, None),
        P("freq", "shot", None, None, None),
        P("shot", None, "freq"),
    )
    body = functools.partial(local, mesh.shape["freq"], mesh.shape["shot"])
    return jax.shard_map(body, mesh=mesh, in_specs=in_specs, out_specs=out_specs, check_vma=False)
```

```python
import functools
import math

import jax
import jax.numpy as jnp
from jax import lax
from jax.experimental import pallas as pl
from jax.experimental.pallas import tpu as pltpu
from jax.sharding import PartitionSpec as P

DEPTH = 2
TILE_DEV = 4
CHUNK = 256
LAST_CHUNK = 1024
WHOLE = 12582912.0
SIN = (4.44288292, -7.3082457, 3.60635441, -0.84611287, 0.10982695)
COS = (1.4142135, -6.97885099, 5.73946116, -1.88356292, 0.31069804)
F32 = jnp.float32
BF16 = jnp.bfloat16
MESH = pl.DeviceIdType.MESH
HOP = 2
PLANE = 2
CORE = 2


def horner(coefficients, z):
    total = jnp.full_like(z, coefficients[-1])
    for coefficient in coefficients[-2::-1]:
        total = total * z + coefficient
    return total


def cos_sin(turns):
    r = turns - ((turns + WHOLE) - WHOLE)
    z = r * r
    half_sin = r * horner(SIN, z)
    half_cos = horner(COS, z)
    return 1.0 - half_sin * half_sin, half_sin * half_cos


def pair_matrix(real, below_left, above_right):
    return jnp.concatenate(
        [jnp.concatenate([real, above_right], axis=1), jnp.concatenate([below_left, real], axis=1)], axis=0
    )


def x_matrix(x_ref, f):
    return pair_matrix(x_ref[f, 0], -x_ref[f, 1], x_ref[f, 1])


def y_matrix(y_ref, f):
    real = y_ref[f, 0].astype(F32).T.astype(BF16)
    imag = y_ref[f, 1].astype(F32).T.astype(BF16)
    return pair_matrix(real, imag, -imag)


def sweep_x(re, im, mx):
    rows = jnp.concatenate(
        [
            jnp.concatenate([re[:, t : t + 128], im[:, t : t + 128]], axis=1)
            for t in range(0, re.shape[1], 128)
        ],
        axis=0,
    )
    swept = (rows.astype(F32) + jnp.dot(rows, mx, preferred_element_type=F32)).astype(BF16)
    height = re.shape[0]
    return [
        jnp.concatenate([swept[t : t + height, c : c + 128] for t in range(0, swept.shape[0], height)], axis=1)
        for c in (0, 128)
    ]


def sweep_y(re, im, my):
    columns = jnp.concatenate([re, im], axis=0)
    out = columns.astype(F32) + jnp.dot(my, columns, preferred_element_type=F32)
    return out[: re.shape[0]], out[re.shape[0] :]


def last_kernel(
    freq_total, ids_ref, y_ref, source_ref, receiver_ref, first_source, first_receiver, half_source, half_receiver,
    source_out, receiver_out, term_ref, my, tiles, tile_sem,
):
    step = pl.program_id(0)
    aper = term_ref.shape[0]
    tile_width = term_ref.shape[-1]
    share = 128 // tile_width
    whole = ((first_source, first_receiver), (half_source, half_receiver))

    def loads(a):
        at = pl.ds(pl.multiple_of(ids_ref[a] // share * 128, 128), 128)
        return [
            pltpu.make_async_copy(
                whole[d][field].at[:, 0, :, :, at], tiles.at[a, d, field], tile_sem.at[a, d, field]
            )
            for d in range(DEPTH)
            for field in range(2)
        ]

    @pl.when(step == 0)
    def _():
        for a in range(aper):
            for load in loads(a):
                load.start()
        for f in range(y_ref.shape[0]):
            my[f] = y_matrix(y_ref, f)

    for f in range(source_ref.shape[0]):
        re, im = sweep_y(source_ref[f, 0, 0], source_ref[f, 0, 1], my[f])
        source_out[f, 0, 0] = re.astype(BF16)
        source_out[f, 0, 1] = im.astype(BF16)
        re, im = sweep_y(receiver_ref[f, 0, 0], receiver_ref[f, 0, 1], my[f])
        receiver_out[f, 0, 0] = re.astype(BF16)
        receiver_out[f, 0, 1] = (-im).astype(BF16)

    @pl.when(step == 1)
    def _():
        for a in range(aper):
            for load in loads(a):
                load.wait()
            place = ids_ref[a] % share
            for d in range(DEPTH):
                total = jnp.zeros((term_ref.shape[2], 128), F32)
                for f in range(source_ref.shape[0]):
                    re, im = [
                        jnp.concatenate([tiles[a, d, field, f, part] for field in range(2)], axis=1)
                        for part in range(2)
                    ]
                    if d == DEPTH - 1:
                        re, im = [value.astype(BF16) for value in sweep_y(re, im, my[f])]
                    re, im = re.astype(F32), im.astype(F32)
                    total += re[:, :128] * re[:, 128:] - im[:, :128] * im[:, 128:]
                total = total * (1.0 / freq_total)
                picked = total[:, :tile_width]
                for p in range(1, share):
                    picked = jnp.where(place == p, total[:, p * tile_width : (p + 1) * tile_width], picked)
                term_ref[a, d] = picked


def last_sweep(freq_total, tile_total, ids, yc, first_source, first_receiver, source, receiver):
    count, _, _, height, width = source.shape
    aper = ids.shape[0]
    spec = pl.BlockSpec((count, 1, 2, height, LAST_CHUNK), lambda i: (0, 0, 0, 0, i))
    shape = jax.ShapeDtypeStruct(source.shape, BF16)
    term = (aper, DEPTH, height, width // tile_total)
    anywhere = pl.BlockSpec(memory_space=pl.ANY)
    return pl.pallas_call(
        functools.partial(last_kernel, freq_total),
        grid=(width // LAST_CHUNK,),
        in_specs=[
            pl.BlockSpec(memory_space=pltpu.SMEM), pl.BlockSpec(yc.shape, lambda i: (0, 0, 0, 0)),
            spec, spec, anywhere, anywhere, anywhere, anywhere,
        ],
        out_specs=[spec, spec, pl.BlockSpec(term, lambda i: (0, 0, 0, 0))],
        out_shape=[shape, shape, jax.ShapeDtypeStruct(term, F32)],
        scratch_shapes=[
            pltpu.VMEM((count, 256, 256), BF16),
            pltpu.VMEM((aper, DEPTH, 2, count, 2, height, 128), BF16),
            pltpu.SemaphoreType.DMA((aper, DEPTH, 2)),
        ],
        compiler_params=pltpu.CompilerParams(vmem_limit_bytes=60 * 2**20),
        name="last_sweep",
    )(ids, yc, source, receiver, first_source, first_receiver, source, receiver)


def greet(devices, count):
    barrier = pltpu.get_barrier_semaphore()
    for there, device in devices:
        if there is None:
            pl.semaphore_signal(barrier, inc=1, device_id=device, device_id_type=MESH)
        else:

            @pl.when(there)
            def _(device=device):
                pl.semaphore_signal(barrier, inc=1, device_id=device, device_id_type=MESH)

    pl.semaphore_wait(barrier, count)


def remote(src, dst, send, recv, device):
    return pltpu.make_async_remote_copy(
        src_ref=src, dst_ref=dst, send_sem=send, recv_sem=recv, device_id=device, device_id_type=MESH
    )


def slab_kernel(
    freqs, shots, owner_ref, freq_ref, velocity_ref, source_ref, receiver_ref, x_ref, y_ref,
    source_first, receiver_first, source_out, receiver_out,
    slabs, own_part, sibling_part, mine, up_out, up_in, down_out, down_in, fields, stage, mx, my,
    pair_sem, up_sem, down_sem, plane_send, plane_recv, core_send, core_recv, in_sem, out_sem,
):
    f = lax.axis_index("freq")
    s = lax.axis_index("shot")
    chain = shots // 2
    z = s // 2
    c = s % 2
    rows, width = slabs.shape[2], slabs.shape[3]
    chunks = width // CHUNK
    sibling = (f, z * 2 + 1 - c)
    above = (f, jnp.minimum(s + 2, shots - 2 + c))
    below = (f, jnp.maximum(s - 2, c))
    own = f * 2 + c
    field_refs = (source_ref, receiver_ref)
    out_refs = (source_first, receiver_first, source_out, receiver_out)
    count, height = source_ref.shape[0], source_ref.shape[3]
    loads = [
        pltpu.make_async_copy(field_refs[i].at[:, 0], fields.at[i], in_sem.at[i]) for i in range(2)
    ]
    others = [(lax.rem(f + j, freqs), s) for j in range(1, freqs)]
    has_below = z > 0
    has_above = z < chain - 1
    greet(
        [(None, sibling)] + [(None, o) for o in others] + [(has_above, above), (has_below, below)],
        freqs + has_above.astype(jnp.int32) + has_below.astype(jnp.int32),
    )

    def row_slice(index):
        return pl.ds(pl.multiple_of(index * rows, 8), rows)

    pair = remote(
        velocity_ref.at[0, row_slice(f * 2 + 1 - c)], sibling_part, pair_sem.at[0], pair_sem.at[1], sibling
    )
    pair.start()
    own_load = pltpu.make_async_copy(velocity_ref.at[0, row_slice(own)], own_part, in_sem.at[2])
    own_load.start()
    for load in loads:
        load.start()
    for i in range(count):
        mx[i] = x_matrix(x_ref, i)
        my[i] = y_matrix(y_ref, i)

    @pl.when(z == 0)
    def _():
        up_in[...] = jnp.zeros_like(up_in)

    @pl.when(z == chain - 1)
    def _():
        down_in[...] = jnp.zeros_like(down_in)

    own_load.wait()
    pair.wait_recv()
    here = own_part[...]
    there = sibling_part[...]
    for d in range(DEPTH):
        held = jnp.where(owner_ref[d] == s, here, jnp.zeros_like(here))
        mine[d] = jnp.where(owner_ref[d] == z * 2 + 1 - c, there, held)

    def at(k):
        return pl.ds(pl.multiple_of(k * CHUNK, CHUNK), CHUNK)

    def up_copy(k):
        return remote(
            up_out.at[:, :, at(k)], up_in.at[:, :, at(k)], up_sem.at[0, k], up_sem.at[1, k], above
        )

    def down_copy(k):
        return remote(
            down_out.at[:, :, at(k)], down_in.at[:, :, at(k)], down_sem.at[0, k], down_sem.at[1, k], below
        )

    def plane_copy(j, k):
        place = slabs.at[:, own, :, at(k)]
        return remote(place, place, plane_send.at[j - 1, k], plane_recv.at[j - 1, k], others[j - 1])

    def core_copy(j, k):
        place = slabs.at[:, lax.rem(f + freqs - j, freqs) * 2 + c, :, at(k)]
        return remote(place, place, core_send.at[j, k], core_recv.at[j, k], sibling)

    def arrived(j, k):
        place = slabs.at[:, lax.rem(f + freqs - j, freqs) * 2 + c, :, at(k)]
        return remote(place, place, plane_send.at[j - 1, k], plane_recv.at[j - 1, k], others[j - 1])

    def core_arrived(j, k):
        place = slabs.at[:, lax.rem(f + freqs - j, freqs) * 2 + 1 - c, :, at(k)]
        return remote(place, place, core_send.at[j, k], core_recv.at[j, k], sibling)

    def go_up(k):
        @pl.when(has_below)
        def _():
            up_copy(k).wait_recv()

        @pl.when(has_above)
        def _():
            up_out[:, :, at(k)] = up_in[:, :, at(k)] + mine[:, :, at(k)]
            up_copy(k).start()

    def go_down(k):
        @pl.when(has_above)
        def _():
            down_copy(k).wait_recv()

        @pl.when(has_below)
        def _():
            down_out[:, :, at(k)] = down_in[:, :, at(k)] + mine[:, :, at(k)]
            down_copy(k).start()

    z_lag = HOP * (chain - 1)
    plane_lag = z_lag + PLANE
    core_lag = plane_lag + CORE

    def out_copy(i, k):
        held = fields if i < 2 else stage
        return pltpu.make_async_copy(
            held.at[i % 2, :, :, :, at(k)], out_refs[i].at[:, 0, :, :, at(k)], out_sem.at[i, k]
        )

    def compute(k):
        for i in range(count):
            scale = freq_ref[i] * (0.5 / math.pi)
            cosine, sine = cos_sin(slabs[0, :, :, at(k)].reshape(height, CHUNK) * scale)
            sre, sim, rre, rim = [
                fields[field, i, part, :, at(k)].astype(F32) for field in range(2) for part in range(2)
            ]
            re = jnp.concatenate([sre * cosine - sim * sine, rre * cosine + rim * sine], axis=1)
            im = jnp.concatenate([sre * sine + sim * cosine, rre * sine - rim * cosine], axis=1)
            re, im = sweep_y(*sweep_x(re.astype(BF16), im.astype(BF16), mx[i]), my[i])
            re, im = re.astype(BF16), im.astype(BF16)
            for field in range(2):
                fields[field, i, 0, :, at(k)] = re[:, field * CHUNK : (field + 1) * CHUNK]
                fields[field, i, 1, :, at(k)] = im[:, field * CHUNK : (field + 1) * CHUNK]
            cosine, sine = cos_sin(slabs[1, :, :, at(k)].reshape(height, CHUNK) * scale)
            cosine = jnp.concatenate([cosine, cosine], axis=1)
            sine = jnp.concatenate([sine, sine], axis=1)
            re, im = re.astype(F32), im.astype(F32)
            re, im = sweep_x(
                (re * cosine - im * sine).astype(BF16), (re * sine + im * cosine).astype(BF16), mx[i]
            )
            for field in range(2):
                stage[field, i, 0, :, at(k)] = re[:, field * CHUNK : (field + 1) * CHUNK]
                stage[field, i, 1, :, at(k)] = im[:, field * CHUNK : (field + 1) * CHUNK]

    def step(i, carry):
        for first, go in ((HOP * z, go_up), (HOP * (chain - 1 - z), go_down)):

            @pl.when(jnp.logical_and(i >= first, i < chunks + first))
            def _(first=first, go=go):
                go(i - first)

        @pl.when(jnp.logical_and(i >= z_lag, i < chunks + z_lag))
        def _():
            k = i - z_lag
            slabs[:, own, :, at(k)] = up_in[:, :, at(k)] + mine[:, :, at(k)] + down_in[:, :, at(k)]
            for j in range(1, freqs):
                plane_copy(j, k).start()
            core_copy(0, k).start()

        @pl.when(jnp.logical_and(i >= plane_lag, i < chunks + plane_lag))
        def _():
            k = i - plane_lag
            for j in range(1, freqs):
                arrived(j, k).wait_recv()
                core_copy(j, k).start()

        @pl.when(i == core_lag)
        def _():
            for load in loads:
                load.wait()

        @pl.when(i >= core_lag)
        def _():
            k = i - core_lag
            for j in range(freqs):
                core_arrived(j, k).wait_recv()
            compute(k)
            for out in range(4):
                out_copy(out, k).start()

        return carry

    lax.fori_loop(0, chunks + core_lag, step, 0)
    pair.wait_send()

    def drain(k, carry):
        @pl.when(has_above)
        def _():
            up_copy(k).wait_send()

        @pl.when(has_below)
        def _():
            down_copy(k).wait_send()

        for j in range(1, freqs):
            plane_copy(j, k).wait_send()
        for j in range(freqs):
            core_copy(j, k).wait_send()
        for out in range(4):
            out_copy(out, k).wait()
        return carry

    lax.fori_loop(0, chunks, drain, 0)


def exchange_slabs(freqs, shots, owners, freq, velocity, source, receiver, xc, yc):
    _, height, width = velocity.shape
    count = source.shape[0]
    rows = height // (2 * freqs)
    chunks = width // CHUNK
    vmem = pl.BlockSpec(memory_space=pltpu.VMEM)
    smem = pl.BlockSpec(memory_space=pltpu.SMEM)
    anywhere = pl.BlockSpec(memory_space=pl.ANY)
    strip = pltpu.VMEM((DEPTH, rows, width), F32)
    field = pltpu.VMEM((2, count, 2, height, width), BF16)
    matrix = pltpu.VMEM((count, 256, 256), BF16)
    dma = pltpu.SemaphoreType.DMA
    shape = jax.ShapeDtypeStruct(source.shape, BF16)
    return pl.pallas_call(
        functools.partial(slab_kernel, freqs, shots),
        in_specs=[smem, smem, anywhere, anywhere, anywhere, vmem, vmem],
        out_specs=[anywhere] * 4,
        out_shape=[shape] * 4,
        scratch_shapes=[
            pltpu.VMEM((DEPTH, 2 * freqs, rows, width), F32),
            pltpu.VMEM((rows, width), F32),
            pltpu.VMEM((rows, width), F32),
            strip, strip, strip, strip, strip, field, field, matrix, matrix,
            dma((2,)), dma((2, chunks)), dma((2, chunks)),
            dma((freqs - 1, chunks)), dma((freqs - 1, chunks)),
            dma((freqs, chunks)), dma((freqs, chunks)), dma((3,)), dma((4, chunks)),
        ],
        compiler_params=pltpu.CompilerParams(
            collective_id=0, has_side_effects=True, vmem_limit_bytes=60 * 2**20
        ),
        name="slabs_and_sweeps",
    )(owners, freq, velocity, source, receiver, xc, yc)


def image_kernel(
    freqs, shots, ids_ref, order_ref, term_ref, out_ref,
    landed, gathered, sum_send, sum_recv, shot_send, shot_recv, core_send, core_recv,
):
    f = lax.axis_index("freq")
    s = lax.axis_index("shot")
    chain = shots // 2
    z = s // 2
    c = s % 2
    aper = term_ref.shape[0]
    rows = out_ref.shape[2]
    sibling = (f, z * 2 + 1 - c)
    others = [(lax.rem(f + j, freqs), s) for j in range(1, freqs)]
    chips = [lax.rem(z + j, chain) * 2 + c for j in range(chain)]
    greet(
        [(None, sibling)] + [(None, o) for o in others] + [(None, (f, chip)) for chip in chips[1:]],
        freqs + chain - 1,
    )

    def row_slice(index):
        return pl.ds(pl.multiple_of(index * rows, 8), rows)

    sums = [
        remote(
            term_ref.at[:, :, row_slice(others[j - 1][0])], landed.at[j - 1],
            sum_send.at[j - 1], sum_recv.at[j - 1], others[j - 1],
        )
        for j in range(1, freqs)
    ]
    for copy in sums:
        copy.start()
    for a in range(aper):
        gathered[s, a, DEPTH * rows :] = jnp.full((8, term_ref.shape[3]), ids_ref[a].astype(F32))
    total = term_ref[:, :, row_slice(f)]
    for j in range(1, freqs):
        sums[j - 1].wait_recv()
        total = total + landed[j - 1]
    gathered[s, :, : DEPTH * rows] = total.reshape(aper, DEPTH * rows, -1)

    place = gathered.at[s]
    sends = [
        remote(place, place, shot_send.at[j - 1], shot_recv.at[j - 1], (f, chips[j])) for j in range(1, chain)
    ]
    for copy in sends:
        copy.start()
    forwards = []
    for j in range(chain):
        source = gathered.at[lax.rem(z + chain - j, chain) * 2 + c]
        if j:
            remote(source, source, shot_send.at[j - 1], shot_recv.at[j - 1], (f, chips[j])).wait_recv()
        forwards.append(remote(source, source, core_send.at[j], core_recv.at[j], sibling))
        forwards[-1].start()
    for j in range(chain):
        landing = gathered.at[lax.rem(z + chain - j, chain) * 2 + 1 - c]
        remote(landing, landing, core_send.at[j], core_recv.at[j], sibling).wait_recv()

    for p in range(TILE_DEV):
        wanted = order_ref[s * TILE_DEV + p].astype(F32)
        picked = jnp.zeros((DEPTH * rows // 8, 8, term_ref.shape[3]), F32)
        for other in range(shots):
            for a in range(aper):
                hit = gathered[other, a, DEPTH * rows :] == wanted
                value = gathered[other, a, : DEPTH * rows].reshape(picked.shape)
                picked += jnp.where(hit[None], value, 0.0)
        out_ref[p] = picked.reshape(DEPTH, rows, -1)
    for copy in sums + sends + forwards:
        copy.wait_send()


def exchange_image(freqs, shots, ids, order, terms):
    aper, _, height, tile_width = terms.shape
    rows = height // freqs
    chain = shots // 2
    smem = pl.BlockSpec(memory_space=pltpu.SMEM)
    vmem = pl.BlockSpec(memory_space=pltpu.VMEM)
    dma = pltpu.SemaphoreType.DMA
    image = pl.pallas_call(
        functools.partial(image_kernel, freqs, shots),
        in_specs=[smem, smem, vmem],
        out_specs=vmem,
        out_shape=jax.ShapeDtypeStruct((TILE_DEV, DEPTH, rows, tile_width), F32),
        scratch_shapes=[
            pltpu.VMEM((freqs - 1, aper, DEPTH, rows, tile_width), F32),
            pltpu.VMEM((shots, aper, DEPTH * rows + 8, tile_width), F32),
            dma((freqs - 1,)), dma((freqs - 1,)), dma((chain - 1,)), dma((chain - 1,)),
            dma((chain,)), dma((chain,)),
        ],
        compiler_params=pltpu.CompilerParams(
            collective_id=1, has_side_effects=True, vmem_limit_bytes=60 * 2**20
        ),
        name="exchange_image",
    )(ids, order, terms)
    return image.reshape(TILE_DEV, DEPTH, rows * tile_width)


def local(
    freqs, shots, source_field, receiver_field, angular_freq, x_correction, y_correction,
    velocity, slab_owner, apertures, tile_order,
):
    tile_ids = apertures[0]
    first_source, first_receiver, source, receiver = exchange_slabs(
        freqs, shots, slab_owner, angular_freq, velocity, source_field, receiver_field,
        x_correction, y_correction,
    )
    source, receiver, terms = last_sweep(
        angular_freq.shape[0] * freqs, tile_order.shape[0],
        tile_ids, y_correction, first_source, first_receiver, source, receiver,
    )
    return source, receiver, exchange_image(freqs, shots, tile_ids, tile_order, terms)


def solution(mesh):
    in_specs = (
        P("freq", "shot", None, None, None),
        P("freq", "shot", None, None, None),
        P("freq"),
        P("freq", None, None, None),
        P("freq", None, None, None),
        P("shot", None, None),
        P(),
        P("shot", None),
        P(),
    )
    out_specs = (
        P("freq", "shot", None, None, None),
        P("freq", "shot", None, None, None),
        P("shot", None, "freq"),
    )
    body = functools.partial(local, mesh.shape["freq"], mesh.shape["shot"])
    return jax.shard_map(body, mesh=mesh, in_specs=in_specs, out_specs=out_specs, check_vma=False)
```
